256 devices in a mesh: blk: 16 (over y, x_lo, core), grp: 16 (over z, x_hi).
Axes of the slice: x: 4 (x_hi: 2, x_lo: 2; x = x_hi * 2 + x_lo), y: 4, z: 8, core: 2. Of those that a mesh axis runs over, the one named last changes fastest.
Arguments:
- series: bfloat16 [32768, 2048], P(('blk', 'grp')), may hold values from -24 to 24
- positives: bfloat16 [32768, 256], P(('blk', 'grp')), may hold values from -6 to 6
- w_last: bfloat16 [2048, 4096], P(None, 'grp'), may hold values from -0.125 to 0.125
- w_head: bfloat16 [4096, 256], P('grp'), may hold values from -0.09375 to 0.09375
- pair_index: int32 [32768], P('blk'), may hold values from 0 to 32767, each once
Outputs:
- mean_loss: float32 [], replicated
- grad_last: float32 [2048, 4096], P('blk', 'grp')
- grad_head: float32 [4096, 256], P('grp', 'blk')
The draws below stay inside these ranges and needn't reach their ends.
Inputs may be any that keep to these rules, and one draw needn't show every extreme that they name: A permutation of the rows: series i is paired with row pair_index[i] of positives.
All inputs are finite; a program needn't handle non-finite values.
Results may differ from the reference program's by a relative error of at most 0.0035.
The reference program's roundings to bfloat16 on the way count: a program that leaves them out, or rounds other values in their place, can miss the bound.
Values may be sent and summed in bfloat16 or wider, within the bound.
A program may use at most 64 MiB of HBM per device.

```python
import jax
import jax.numpy as jnp
from jax import lax

D = 2048
H = 4096
E = 256
TOKENS = 32768


def strengthened(drawn, own_key, source, target, parts, factor):
    def block_of(dim):
        return (jnp.arange(drawn.shape[dim]) // (drawn.shape[dim] // parts)).reshape((-1,) + (1,) * (drawn.ndim - 1 - dim))

    first = jax.random.permutation(own_key, parts)[block_of(target)]
    other_side = (block_of(target) + parts // 2) % parts
    return jnp.where((block_of(source) == first) | (block_of(source) == other_side), factor * drawn, drawn)


def block_levels(key, dims, cuts, low, high):
    loudness = 1.0
    for position, shards_of in cuts:
        heights = jax.random.uniform(jax.random.fold_in(jax.random.fold_in(key, 6), position), (shards_of,), jnp.float32, low / len(cuts), high / len(cuts))
        loudness = loudness * jnp.repeat(jnp.exp(heights), dims[position] // shards_of).reshape((-1,) + (1,) * (len(dims) - 1 - position))
    return loudness


def scatter_about(own_key, dims, scale, most, cuts=(), kind=jnp.bfloat16):
    entries = jax.random.normal(own_key, dims, jnp.float32) * scale
    if len(cuts) > 0:
        entries = block_levels(own_key, dims, cuts, -0.22, 0.18) * entries
    return jnp.clip(entries, min=-most, max=most).astype(kind)


def heavy_noise(own_key, dims, scale, reach, shards, heavy, held_as=jnp.bfloat16):
    result = scale * jax.random.normal(own_key, dims, jnp.float32)
    if shards:
        result = result * block_levels(own_key, dims, shards, -0.22, 0.18)
    return jnp.clip(strengthened(result, jax.random.fold_in(own_key, 3), *heavy), -reach, reach).astype(held_as)


def setup_inputs(seed: int = 0) -> dict:
    key_list = jax.random.split(jax.random.key(seed), 6)
    return {
        "series": heavy_noise(key_list[0], (TOKENS, D), 1.0, 24.0, ((0, 256),), (0, 1, 256, 6.0)),
        "positives": scatter_about(key_list[1], (TOKENS, E), 1.0, 6.0, ((0, 256),)),
        "w_last": scatter_about(key_list[2], (D, H), D ** -0.5, 0.125, ((1, 16),)),
        "w_head": scatter_about(key_list[3], (H, E), H ** -0.5, 0.09375, ((0, 16),)),
        "pair_index": jax.random.permutation(key_list[4], TOKENS).astype(jnp.int32),
    }


SOFTMAX_TEMP_SCALE = 0.05
EPSILON = 1e-06

def reference(series, positives, w_last, w_head, pair_index):
    tokens = series.shape[0]
    block_rows = min(1024, tokens)
    block_count = tokens // block_rows
    series_blocks = series.reshape(block_count, block_rows, series.shape[1])
    pair_blocks = pair_index.reshape(block_count, block_rows)

    def encode(series_blk):
        preact = jnp.dot(series_blk, w_last, preferred_element_type=jnp.float32)
        hidden = jax.nn.gelu(preact).astype(jnp.bfloat16)
        head_sum = jnp.dot(hidden, w_head, preferred_element_type=jnp.float32)
        row_norm = jnp.sqrt(lax.optimization_barrier(jnp.sum(head_sum * head_sum, axis=1, keepdims=True)) + EPSILON)
        return (head_sum / row_norm, row_norm)
    unit_blocks, norm_blocks = lax.map(encode, series_blocks)
    key_float = positives.astype(jnp.float32)
    key_norm = jnp.sqrt(lax.optimization_barrier(jnp.sum(key_float * key_float, axis=1, keepdims=True)) + EPSILON)
    unit_key_rows = (key_float / key_norm).astype(jnp.bfloat16)
    key_index = jnp.arange(tokens, dtype=jnp.int32)

    def contrast(inputs):
        unit_rows, row_norm, pair_blk = inputs
        query_matrix = unit_rows.astype(jnp.bfloat16)
        score_matrix = lax.dot_general(query_matrix, unit_key_rows, (((1,), (1,)), ((), ())), preferred_element_type=jnp.float32) / SOFTMAX_TEMP_SCALE
        exp_terms = jnp.exp(score_matrix)
        exponent_total = lax.optimization_barrier(jnp.sum(exp_terms, axis=1))
        is_pair = pair_blk[:, None] == key_index[None, :]
        pair_score = lax.optimization_barrier(jnp.sum(jnp.where(is_pair, score_matrix, 0.0), axis=1))
        weighted_keys = jnp.dot(exp_terms.astype(jnp.bfloat16), unit_key_rows, preferred_element_type=jnp.float32)
        matched_scores = jnp.take(unit_key_rows, pair_blk, axis=0).astype(jnp.float32)
        unit_gradient = (weighted_keys / exponent_total[:, None] - matched_scores) / SOFTMAX_TEMP_SCALE
        along = lax.optimization_barrier(jnp.sum(unit_rows * unit_gradient, axis=1, keepdims=True))
        grad_rows = ((unit_gradient - unit_rows * along) / row_norm).astype(jnp.bfloat16)
        return (jnp.log(exponent_total) - pair_score, grad_rows)
    row_loss, grad_blocks = lax.map(contrast, (unit_blocks, norm_blocks, pair_blocks))

    def backward(running, inputs):
        series_blk, grad_rows = inputs
        preact = jnp.dot(series_blk, w_last, preferred_element_type=jnp.float32)
        hidden = jax.nn.gelu(preact).astype(jnp.bfloat16)
        d_hidden = lax.dot_general(grad_rows, w_head, (((1,), (1,)), ((), ())), preferred_element_type=jnp.float32)
        d_preact = jax.vjp(jax.nn.gelu, preact)[1](d_hidden)[0].astype(jnp.bfloat16)
        grad_last = running[0] + lax.dot_general(series_blk, d_preact, (((0,), (0,)), ((), ())), preferred_element_type=jnp.float32)
        grad_head = running[1] + lax.dot_general(hidden, grad_rows, (((0,), (0,)), ((), ())), preferred_element_type=jnp.float32)
        return ((grad_last, grad_head), None)
    start_value = (jnp.zeros((w_last.shape[0], w_last.shape[1]), jnp.float32), jnp.zeros((w_head.shape[0], w_head.shape[1]), jnp.float32))
    (grad_last, grad_head), unused = lax.scan(backward, start_value, (series_blocks, grad_blocks))
    mean_loss = jnp.sum(row_loss) / tokens
    return (mean_loss, grad_last, grad_head)
```

```python
import math
import types

import jax
import jax.numpy as jnp
from jax import lax
from jax.experimental import pallas as pl
from jax.experimental.pallas import tpu as pltpu
from jax.sharding import PartitionSpec as P

MESH = pl.DeviceIdType.MESH
F32 = jnp.float32
BF16 = jnp.bfloat16

TEMP = 0.05
EPSILON = 1e-06
GELU_A = math.sqrt(2.0 / math.pi)
GELU_B = 0.044715
VMEM_BYTES = 56 * 1024 * 1024


def dot_nn(left, right):
    return lax.dot_general(left, right, (((1,), (0,)), ((), ())), preferred_element_type=F32)


def dot_nt(left, right):
    return lax.dot_general(left, right, (((1,), (1,)), ((), ())), preferred_element_type=F32)


def fold_lanes(x):
    total = x[:, 0:128]
    for k in range(1, x.shape[1] // 128):
        total = total + x[:, k * 128 : (k + 1) * 128]
    return total


def kernel(dims, refs_in, refs_out, refs):
    Z, PL, TB, D, HS, E, TOKENS = dims
    series, positives, w_last, w_head, pair = refs_in
    loss_out, gl_out, gh_out = refs_out
    r = refs
    U = PL // 2
    HALF = TB // 2
    UNIT = 2 * TB
    KEYS = 2 * Z * TB
    DS = D // PL
    ES = E // PL
    GRP_ROWS = 2 * Z * TB
    J = Z - 1
    blk = lax.axis_index("blk")
    grp = lax.axis_index("grp")
    core = blk % 2
    other = 1 - core
    xhi = grp % 2
    z = grp // 2
    uid = blk // 2
    pid = uid * 2 + xhi
    sib_dev = (uid * 2 + other, grp)
    holder = core == xhi

    def zwrap(v):
        return lax.rem(v + 2 * Z, Z)

    def column(zz):
        return (blk, zz * 2 + xhi)

    def plane(p):
        return ((p // 2) * 2 + core, z * 2 + p % 2)

    def rows_of(zz, c, start=0, size=TB):
        return pl.ds(pl.multiple_of((zz * 2 + c) * TB + start, 16), size)

    def unit_rows_of(u):
        return pl.ds(pl.multiple_of(u * UNIT, UNIT), UNIT)

    def remote(src, dst, ssem, rsem, dev):
        return pltpu.make_async_remote_copy(
            src_ref=src, dst_ref=dst, send_sem=ssem, recv_sem=rsem, device_id=dev, device_id_type=MESH
        )

    def each(low, high, body):
        def step(i, c):
            body(i)
            return c

        lax.fori_loop(low, high, step, 0)

    def unit_z(i):
        half = (i + 1) // 2
        return zwrap(z + half * (1 - 2 * (i % 2)))

    def unit_u(i):
        total = 0
        for b in range(U.bit_length() - 1):
            mine, flip = (uid // (1 << b)) % 2, (i // (1 << b)) % 2
            total = total + (mine + flip - 2 * mine * flip) * (1 << b)
        return total

    barrier = pltpu.get_barrier_semaphore()

    def greet(dev):
        pl.semaphore_signal(barrier, inc=1, device_id=dev, device_id_type=MESH)

    def greet_plane(i):
        p = lax.rem(pid + i, PL)
        greet(plane(p))
        greet(((p // 2) * 2 + xhi, z * 2 + p % 2))

    greet(sib_dev)
    each(1, Z, lambda i: greet(column(zwrap(z + i))))
    each(1, PL, greet_plane)

    own_rows = rows_of(z, core)
    x_copy = pltpu.make_async_copy(series, r.xbuf.at[own_rows], r.x_sem)
    x_copy.start()
    key_float = positives[...].astype(F32)
    key_norm = jnp.sqrt(jnp.sum(key_float * key_float, axis=1, keepdims=True) + EPSILON)
    r.kbuf[own_rows, :] = (key_float / key_norm).astype(BF16)
    r.prbuf[uid] = pair[...]

    pl.semaphore_wait(barrier, 1 + (Z - 1) + (PL - 1) + PL - 2 * jnp.where(holder, 1, 0))

    def key_zz(direction, s):
        return zwrap(z - s) if direction == 0 else zwrap(z + s)

    def key_hops(direction):
        return Z // 2 - direction

    def key_copy(direction, s):
        rows = rows_of(key_zz(direction, s), core)
        dev = column(zwrap(z + 1 - 2 * direction))
        return remote(
            r.kbuf.at[rows], r.kbuf.at[rows], r.k_send.at[direction, s], r.k_recv.at[direction, s], dev
        )

    def key_arrival(direction, s):
        rows = rows_of(key_zz(direction, s), core)
        return remote(
            r.kbuf.at[rows], r.kbuf.at[rows], r.k_send.at[direction, s - 1], r.k_recv.at[direction, s - 1], sib_dev
        )

    def key_sib(direction, s, c):
        rows = rows_of(key_zz(direction, s), c)
        return remote(
            r.kbuf.at[rows], r.kbuf.at[rows], r.ks_send.at[direction, s], r.ks_recv.at[direction, s], sib_dev
        )

    def key_pass(s):
        for direction in (0, 1):
            if s <= key_hops(direction):
                key_arrival(direction, s).wait_recv()
                if s < key_hops(direction):
                    key_copy(direction, s).start()
                key_sib(direction, s, core).start()

    for direction in (0, 1):
        if key_hops(direction) > 0:
            key_copy(direction, 0).start()
    key_sib(0, 0, core).start()

    def ring_rows(direction, j, hops, c):
        s = j // 2 + hops
        h = j % 2 if direction == 0 else 1 - j % 2
        zz = zwrap(z - s) if direction == 0 else zwrap(z + s)
        return rows_of(zz, c, h * HALF, HALF), h

    def ring_copy(direction, j):
        rows, h = ring_rows(direction, j, 0, core)
        src = series.at[pl.ds(h * HALF, HALF)] if j < 2 else r.xbuf.at[rows]
        dev = column(zwrap(z + 1 - 2 * direction))
        return remote(src, r.xbuf.at[rows], r.ring_send.at[direction, j], r.ring_recv.at[direction, j], dev)

    def arrived(direction, j, c, ssem, rsem):
        rows, _ = ring_rows(direction, j, 1, c)
        return remote(r.xbuf.at[rows], r.xbuf.at[rows], ssem.at[direction, j], rsem.at[direction, j], sib_dev)

    def ring_arrival(direction, j):
        return arrived(direction, j, core, r.ring_send, r.ring_recv)

    def sib_copy(direction, j):
        return arrived(direction, j, core, r.sib_send, r.sib_recv)

    def sib_arrival(direction, j):
        return arrived(direction, j, other, r.sib_send, r.sib_recv)

    for j in range(min(2, J)):
        for direction in (0, 1):
            ring_copy(direction, j).start()
    own_copy = remote(series, r.xbuf.at[own_rows], r.own_send, r.own_recv, sib_dev)
    own_copy.start()

    partner = (blk, z * 2 + 1 - xhi)
    w_copies = [
        remote(w_last, r.wbuf, r.w_send.at[0], r.w_recv.at[0], partner),
        remote(w_head, r.whbuf, r.w_send.at[1], r.w_recv.at[1], partner),
    ]

    @pl.when(holder)
    def _():
        for copy in w_copies:
            copy.start()
        pltpu.make_async_copy(w_last, r.wbuf, r.w_recv.at[0]).start()
        pltpu.make_async_copy(w_head, r.whbuf, r.w_recv.at[1]).start()

    def pair_copy(i):
        u = lax.rem(uid + i, U)
        return remote(pair, r.prbuf.at[uid], r.pr_send.at[i], r.pr_recv.at[uid], plane(u * 2 + xhi))

    def pair_arrival(i):
        u = lax.rem(uid + i, U)
        return remote(pair, r.prbuf.at[u], r.pr_send.at[i], r.pr_recv.at[u], sib_dev)

    each(1, U, lambda i: pair_copy(i).start())

    def to_owner(buf, dst, ssem, rsem, p):
        return remote(buf.at[p], dst.at[pid], ssem.at[p], rsem.at[pid], plane(p))

    def from_helper(buf, dst, ssem, rsem, i):
        p = lax.rem(pid + i, PL)
        return remote(buf.at[p], dst.at[p], ssem.at[p], rsem.at[p], sib_dev)

    m_ops = (r.msend, r.mrecv, r.m_send, r.m_recv)

    def send_unit(u, ops):
        for b in (0, 1):
            p = u * 2 + b

            @pl.when(p != pid)
            def _():
                to_owner(*ops, p).start()

    def find_pairs(i):
        u = unit_u(i)
        lanes = lax.broadcasted_iota(jnp.int32, (UNIT, TB), 1)
        both = [jnp.broadcast_to(r.prbuf[u, pl.ds(z * 2 + b, 1), :], (TB, TB)).T for b in (0, 1)]
        both = jnp.concatenate(both, axis=0) - lanes
        total = jnp.zeros((UNIT, E), F32)
        for zz in range(Z):
            base = (blk - core) * GRP_ROWS + (zz * 2 + xhi) * TB
            hot = jnp.concatenate([both == base, both == base + GRP_ROWS], axis=1)
            hot = jnp.where(hot, 1.0, 0.0).astype(BF16)
            total = total + dot_nn(hot, r.kbuf[zz * UNIT : (zz + 1) * UNIT, :])
        for b in (0, 1):
            r.msend[u * 2 + b] = total[b * TB : (b + 1) * TB, :].astype(BF16)
        send_unit(u, m_ops)

    def hs_copy(zz):
        return remote(r.hsend.at[zz], r.hsib.at[zz], r.hs_send.at[zz], r.hs_recv.at[zz], sib_dev)

    def hd_copy(zz):
        return remote(r.hdir.at[zz], r.hrecv.at[z], r.hd_send.at[zz], r.hd_recv.at[z], column(zz))

    def hd_arrival(zz):
        return remote(r.hdir.at[zz], r.hrecv.at[zz], r.hd_send.at[zz], r.hd_recv.at[zz], sib_dev)

    def encode(i):
        zz = unit_z(i)
        rows = unit_rows_of(zz)
        x = dot_nn(r.xbuf[rows, :], r.wbuf[...])
        x2 = x * x
        t = jnp.tanh(GELU_A * (x + GELU_B * (x2 * x)))
        cdf = 0.5 + 0.5 * t
        hidden = (x * cdf).astype(BF16)
        r.hid[rows, :] = hidden
        r.dgelu[rows, :] = cdf + (0.5 * GELU_A) * x * (1.0 - t * t) * (1.0 + (3.0 * GELU_B) * x2)
        r.hp[rows, :] = dot_nn(hidden, r.whbuf[...])
        r.hsend[zz] = r.hp[rows_of(zz, other), :]
        hs_copy(zz).start()

    def head_send(i):
        zz = unit_z(i)
        hs_copy(zz).wait_recv()
        r.hdir[zz] = (r.hp[rows_of(zz, core), :] + r.hsib[zz]).astype(BF16)
        hd_copy(zz).start()

    x_copy.wait()
    key_pass(1)
    key_pass(2)
    for j in range(J):
        for direction in (0, 1):
            ring_arrival(direction, j).wait_recv()
            if j + 2 < J:
                ring_copy(direction, j + 2).start()
            sib_copy(direction, j).start()
        s = j // 2
        if j == 0:
            for k in range(3, Z // 2 + 1):
                key_pass(k)
        elif j == 1:
            each(1, U, lambda i: pair_arrival(i).wait_recv())
            for direction in (0, 1):
                for k in range(direction, key_hops(direction) + 1):
                    key_sib(direction, k, other).wait_recv()
            each(0, U // 2, find_pairs)
        elif j % 2 == 0:
            if j == 2:
                remote(series, r.xbuf.at[rows_of(z, other)], r.own_send, r.own_recv, sib_dev).wait_recv()
                w_copies[0].wait_recv()
                w_copies[1].wait_recv()
            for direction in (0, 1):
                sib_arrival(direction, j - 2).wait_recv()
                sib_arrival(direction, j - 1).wait_recv()
            each(2 * s - 1 if s > 1 else 0, 2 * s + 1, encode)
        else:
            each(2 * s - 1, 2 * s + 1, head_send)
            if j == 3:
                each(U // 2, U, find_pairs)
    for direction in (0, 1):
        sib_arrival(direction, J - 1).wait_recv()
    encode(Z - 1)
    each(Z - 3, Z, head_send)

    hs_copy(z).wait_recv()
    head = r.hp[own_rows, :] + r.hsib[z]
    for i in range(1, Z):
        zz = zwrap(z + i)
        hd_arrival(zz).wait_recv()
        head = head + r.hrecv[zz].astype(F32)
    row_norm = jnp.sqrt(jnp.sum(head * head, axis=1, keepdims=True) + EPSILON)
    unit_rows = head / row_norm
    r.ubuf[...] = unit_rows
    r.rnbuf[...] = jnp.broadcast_to(row_norm, (TB, 128))
    r.qbuf[pid] = unit_rows.astype(BF16)

    def q_copy(p):
        return remote(r.qbuf.at[pid], r.qbuf.at[pid], r.q_send.at[p], r.q_recv.at[pid], plane(p))

    def q_arrival(p):
        return remote(r.qbuf.at[p], r.qbuf.at[p], r.q_send.at[p], r.q_recv.at[p], sib_dev)

    def each_piece(i, body):
        u = unit_u(i)
        for b in (0, 1):
            p = u * 2 + b

            @pl.when(p != pid)
            def _():
                body(p)

    each(0, U, lambda i: each_piece(i, lambda p: q_copy(p).start()))

    CHUNK = min(512, KEYS)
    scale = (1.0 / TEMP) * math.log2(math.e)
    p_ops = (r.psend, r.precv, r.p_send, r.p_recv)
    t_ops = (r.tsend, r.trecv, r.t_send, r.t_recv)

    def attend(i):
        u = unit_u(i)
        each_piece(i, lambda p: q_arrival(p).wait_recv())
        q = r.qbuf[pl.ds(u * 2, 2)].reshape(UNIT, E)
        total = jnp.zeros((UNIT, 128), F32)
        weighted = jnp.zeros((UNIT, E), F32)
        for k in range(KEYS // CHUNK):
            keys = r.kbuf[k * CHUNK : (k + 1) * CHUNK, :]
            e = jnp.exp2(dot_nt(q, keys) * scale)
            total = total + fold_lanes(e)
            weighted = weighted + dot_nn(e.astype(BF16), keys)
        for b in (0, 1):
            part = jnp.sum(total[b * TB : (b + 1) * TB, :].T, axis=0, keepdims=True)
            r.tsend[u * 2 + b] = jnp.broadcast_to(part, (8, TB))
            r.psend[u * 2 + b] = weighted[b * TB : (b + 1) * TB, :].astype(BF16)
        send_unit(u, p_ops)
        send_unit(u, t_ops)

    each(0, U, attend)

    weighted = r.psend[pid].astype(F32)
    totals = r.tsend[pid]
    matched = r.msend[pid].astype(F32)
    for i in range(1, PL):
        p = lax.rem(pid + i, PL)
        from_helper(*m_ops, i).wait_recv()
        matched = matched + r.mrecv[p].astype(F32)
    for i in range(1, PL):
        p = lax.rem(pid + i, PL)
        from_helper(*p_ops, i).wait_recv()
        from_helper(*t_ops, i).wait_recv()
        weighted = weighted + r.precv[p].astype(F32)
        totals = totals + r.trecv[p]

    inv = jnp.broadcast_to(1.0 / totals[0:1, :], (128, TB)).T
    grad = (weighted * jnp.concatenate([inv] * (E // 128), axis=1) - matched) * (1.0 / TEMP)
    unit_rows = r.ubuf[...]
    along = jnp.sum(unit_rows * grad, axis=1, keepdims=True)
    norm = jnp.concatenate([r.rnbuf[...]] * (E // 128), axis=1)
    r.gbuf[own_rows, :] = ((grad - unit_rows * along) / norm).astype(BF16)

    def g_direct(i):
        rows = r.gbuf.at[own_rows]
        return remote(rows, rows, r.gd_send.at[i], r.gd_recv.at[z], column(unit_z(i)))

    def g_direct_arrival(i):
        zz = unit_z(i)
        rows = r.gbuf.at[rows_of(zz, core)]
        return remote(rows, rows, r.gd_send.at[i], r.gd_recv.at[zz], sib_dev)

    def g_sibling(i, c):
        zz = unit_z(i)
        rows = r.gbuf.at[rows_of(zz, c)]
        return remote(rows, rows, r.gs_send.at[zz], r.gs_recv.at[zz], sib_dev)

    g_sibling(0, core).start()
    each(1, Z, lambda i: g_direct(i).start())

    hit = r.qbuf[pid].astype(F32) * matched
    hit = fold_lanes(jnp.sum(hit.reshape(TB // 8, 8, E), axis=0))
    first = lax.broadcasted_iota(jnp.int32, (8, TB), 0) == 0
    r.lplane[pid] = jnp.where(first, jnp.log(totals), 0.0) - hit * (1.0 / TEMP)

    def lp_copy(i):
        rows = r.lplane.at[pid]
        return remote(rows, rows, r.lp_send.at[i], r.lp_recv.at[pid], plane(lax.rem(pid + i, PL)))

    def lp_arrival(i):
        p = lax.rem(pid + i, PL)
        return remote(r.lplane.at[p], r.lplane.at[p], r.lp_send.at[i], r.lp_recv.at[p], sib_dev)

    def lc_copy(i):
        rows = r.lcol.at[z]
        return remote(rows, rows, r.lc_send.at[i], r.lc_recv.at[z], column(zwrap(z + i)))

    def lc_arrival(i):
        zz = zwrap(z + i)
        return remote(r.lcol.at[zz], r.lcol.at[zz], r.lc_send.at[i], r.lc_recv.at[zz], sib_dev)

    def ls_copy(c):
        return remote(r.lsib.at[c], r.lsib.at[c], r.ls_send, r.ls_recv, sib_dev)

    each(1, PL, lambda i: lp_copy(i).start())

    r.ghacc[...] = jnp.zeros((E, HS), F32)

    def back(i):
        @pl.when(i + 1 < Z)
        def _():
            g_direct_arrival(i + 1).wait_recv()
            g_sibling(i + 1, core).start()

        g_sibling(i, other).wait_recv()
        rows = unit_rows_of(unit_z(i))
        g = r.gbuf[rows, :]
        dp = dot_nt(g, r.whbuf[...]) * r.dgelu[rows, :]
        r.dpt[:, rows] = dp.T.astype(BF16)
        gt = g.astype(F32).T.astype(BF16)
        r.ghacc[...] += dot_nn(gt, r.hid[rows, :])

    each(0, Z, back)
    r.ghb[...] = r.ghacc[...].astype(BF16)

    each(1, PL, lambda i: lp_arrival(i).wait_recv())
    loss = r.lplane[0]
    for p in range(1, PL):
        loss = loss + r.lplane[p]
    r.lcol[z] = loss
    each(1, Z, lambda i: lc_copy(i).start())

    def f_copy(d):
        return remote(r.fsend.at[d], r.frecv.at[pid], r.f_send.at[d], r.f_recv.at[pid], (d, z * 2 + core))

    def f_arrival(p):
        return remote(r.frecv.at[p], r.frecv.at[p], r.f_send.at[p], r.f_recv.at[p], sib_dev)

    def last(i):
        n = unit_u(U - 1 - i)
        cols = pl.ds(pl.multiple_of(n * 2 * DS, 2 * DS), 2 * DS)
        part = dot_nn(r.dpt[...], r.xbuf[:, cols]).astype(BF16)
        for k in (0, 1):
            d = n * 2 + k
            r.fsend[d, 0:HS, :] = part[:, k * DS : (k + 1) * DS]
            gh = r.ghb[pl.ds(pl.multiple_of(d * ES, 16), ES), :]
            for c in range(HS // 128):
                r.fsend[d, HS + c * ES : HS + (c + 1) * ES, :] = gh[:, c * 128 : (c + 1) * 128]
            local = jnp.logical_and(holder, d == blk)

            @pl.when(jnp.logical_not(local))
            def _():
                f_copy(d).start()

            @pl.when(local)
            def _():
                pltpu.make_async_copy(r.fsend.at[d], r.frecv.at[pid], r.f_recv.at[pid]).start()

    each(0, U, last)

    each(1, Z, lambda i: lc_arrival(i).wait_recv())
    loss = r.lcol[0]
    for p in range(1, Z):
        loss = loss + r.lcol[p]
    r.lsib[core] = loss
    ls_copy(core).start()

    for direction in (0, 1):
        for j in range(J):
            ring_copy(direction, j).wait_send()
            sib_copy(direction, j).wait_send()
        for s in range(key_hops(direction)):
            key_copy(direction, s).wait_send()
        for s in range(direction, key_hops(direction) + 1):
            key_sib(direction, s, core).wait_send()
    own_copy.wait_send()

    @pl.when(holder)
    def _():
        for copy in w_copies:
            copy.wait_send()

    each(1, U, lambda i: pair_copy(i).wait_send())
    each(0, Z, lambda i: hs_copy(i).wait_send())
    each(1, Z, lambda i: hd_copy(unit_z(i)).wait_send())

    def sent(i):
        p = lax.rem(pid + i, PL)
        q_copy(p).wait_send()
        to_owner(*m_ops, p).wait_send()
        to_owner(*p_ops, p).wait_send()
        to_owner(*t_ops, p).wait_send()
        lp_copy(i).wait_send()

    each(1, PL, sent)
    each(0, Z, lambda i: g_sibling(i, core).wait_send())
    each(1, Z, lambda i: g_direct(i).wait_send())
    each(1, Z, lambda i: lc_copy(i).wait_send())

    each(0, PL, lambda i: f_arrival(i).wait_recv())
    total = r.frecv[0].astype(F32)
    for p in range(1, PL):
        total = total + r.frecv[p].astype(F32)
    gl_out[...] = total[0:HS, :].T
    gh = jnp.concatenate([total[HS + c * ES : HS + (c + 1) * ES, :] for c in range(HS // 128)], axis=1)
    pad = jnp.concatenate([gh, jnp.zeros((128 - ES, HS), F32)], axis=0) if ES < 128 else gh
    gh_out[...] = pad.T[:, 0:ES]

    ls_copy(other).wait_recv()
    ls_copy(core).wait_send()
    loss = r.lsib[0] + r.lsib[1]
    loss = jnp.sum(loss, axis=1, keepdims=True)
    loss = jnp.sum(loss, axis=0, keepdims=True) * (1.0 / TOKENS)
    loss_out[...] = jnp.broadcast_to(loss, (8, 128))

    def f_sent(d):
        @pl.when(jnp.logical_not(jnp.logical_and(holder, d == blk)))
        def _():
            f_copy(d).wait_send()

    each(0, PL, f_sent)


def solution(mesh):
    PL = mesh.shape["blk"]
    Z = mesh.shape["grp"] // 2
    M = 2 * Z

    def on_device(series, positives, w_last, w_head, pair_index):
        TB, D = series.shape
        HS = w_last.shape[1]
        E = w_head.shape[1]
        J = Z - 1
        DS, ES = D // PL, E // PL
        dims = (Z, PL, TB, D, HS, E, TB * PL * M)
        pair = pair_index.reshape(M, TB)
        vm, sem = pltpu.VMEM, pltpu.SemaphoreType.DMA
        rows = M * TB
        fr = HS + ES * (HS // 128)
        scratch = dict(
            xbuf=vm((rows, D), BF16),
            wbuf=vm((D, HS), BF16),
            whbuf=vm((HS, E), BF16),
            kbuf=vm((rows, E), BF16),
            prbuf=vm((PL // 2, M, TB), jnp.int32),
            msend=vm((PL, TB, E), BF16),
            mrecv=vm((PL, TB, E), BF16),
            hid=vm((rows, HS), BF16),
            dgelu=vm((rows, HS), F32),
            hp=vm((rows, E), F32),
            hsend=vm((Z, TB, E), F32),
            hsib=vm((Z, TB, E), F32),
            hdir=vm((Z, TB, E), BF16),
            hrecv=vm((Z, TB, E), BF16),
            ubuf=vm((TB, E), F32),
            rnbuf=vm((TB, 128), F32),
            qbuf=vm((PL, TB, E), BF16),
            psend=vm((PL, TB, E), BF16),
            precv=vm((PL, TB, E), BF16),
            tsend=vm((PL, 8, TB), F32),
            trecv=vm((PL, 8, TB), F32),
            gbuf=vm((rows, E), BF16),
            dpt=vm((HS, rows), BF16),
            ghacc=vm((E, HS), F32),
            ghb=vm((E, HS), BF16),
            fsend=vm((PL, fr, DS), BF16),
            frecv=vm((PL, fr, DS), BF16),
            lplane=vm((PL, 8, 128), F32),
            lcol=vm((Z, 8, 128), F32),
            lsib=vm((2, 8, 128), F32),
            x_sem=sem,
            own_send=sem,
            own_recv=sem,
            ls_send=sem,
            ls_recv=sem,
        )
        for name, shape in dict(
            ring=(2, J), sib=(2, J), k=(2, Z // 2 + 1), ks=(2, Z // 2 + 1), w=(2,), pr=(PL // 2,), m=(PL,),
            hs=(Z,), hd=(Z,), q=(PL,), p=(PL,), t=(PL,), gd=(Z,), gs=(Z,), lp=(PL,), lc=(Z,), f=(PL,),
        ).items():
            scratch[name + "_send"] = sem(shape)
            scratch[name + "_recv"] = sem(shape)
        names = list(scratch)

        def body(*refs):
            kernel(dims, refs[:5], refs[5:8], types.SimpleNamespace(**dict(zip(names, refs[8:]))))

        any_spec = pl.BlockSpec(memory_space=pl.ANY)
        vm_spec = pl.BlockSpec(memory_space=pltpu.VMEM)
        loss, grad_last, grad_head = pl.pallas_call(
            body,
            out_shape=(
                jax.ShapeDtypeStruct((8, 128), F32),
                jax.ShapeDtypeStruct((DS, HS), F32),
                jax.ShapeDtypeStruct((HS, ES), F32),
            ),
            in_specs=[any_spec, vm_spec, any_spec, any_spec, vm_spec],
            out_specs=(vm_spec, vm_spec, vm_spec),
            scratch_shapes=list(scratch.values()),
            compiler_params=pltpu.CompilerParams(
                collective_id=0, has_side_effects=True, vmem_limit_bytes=VMEM_BYTES
            ),
        )(series, positives, w_last, w_head, pair)
        return (loss[0, 0], grad_last, grad_head)

    return jax.shard_map(
        on_device,
        mesh=mesh,
        in_specs=(
            P(("blk", "grp"), None),
            P(("blk", "grp"), None),
            P(None, "grp"),
            P("grp", None),
            P("blk"),
        ),
        out_specs=(P(), P("blk", "grp"), P("grp", "blk")),
        check_vma=False,
    )
```

```python
import functools
import math
import types

import jax
import jax.numpy as jnp
from jax import lax
from jax.experimental import pallas as pl
from jax.experimental.pallas import tpu as pltpu
from jax.sharding import PartitionSpec as P

MESH = pl.DeviceIdType.MESH
F32 = jnp.float32
BF16 = jnp.bfloat16

TEMP = 0.05
EPSILON = 1e-06
GELU_A = math.sqrt(2.0 / math.pi)
GELU_B = 0.044715
KEY_CHUNKS = 2
CHUNKS = (2, 4)
VMEM_BYTES = 56 * 1024 * 1024


def dot_nn(left, right):
    return lax.dot_general(left, right, (((1,), (0,)), ((), ())), preferred_element_type=F32)


def dot_nt(left, right):
    return lax.dot_general(left, right, (((1,), (1,)), ((), ())), preferred_element_type=F32)


def fold_lanes(x):
    total = x[:, 0:128]
    for k in range(1, x.shape[1] // 128):
        total = total + x[:, k * 128 : (k + 1) * 128]
    return total


def kernel(dims, refs_in, refs_out, refs):
    Z, PL, TB, D, HS, E, TOKENS = dims
    series, positives, w_last, w_head, pair = refs_in
    loss_out, gl_out, gh_out = refs_out
    r = refs
    U = PL // 2
    HOPS = Z // 2
    PT = TB // 2
    PART = 2 * Z * PT
    QUAD = 4 * PT
    KEYS = 2 * Z * TB
    DS = D // PL
    ES = E // PL
    GRP_ROWS = 2 * Z * TB
    blk = lax.axis_index("blk")
    grp = lax.axis_index("grp")
    core = blk % 2
    xhi = grp % 2
    z = grp // 2
    uid = blk // 2
    pid = uid * 2 + xhi
    sib_blk = uid * 2 + 1 - core
    sib_dev = (sib_blk, grp)
    holder = core == xhi

    UB = U.bit_length() - 1
    ubits = [(uid // (1 << b)) % 2 for b in range(UB)]

    def flip(bit, by):
        if isinstance(by, int):
            return 1 - bit if by else bit
        return bit + by - 2 * bit * by

    def bits_of(j, count):
        if isinstance(j, int):
            return [(j >> b) & 1 for b in range(count)]
        out = []
        for b in reversed(range(count)):
            bit = jnp.where(j >= (1 << b), 1, 0)
            out.append(bit)
            j = j - bit * (1 << b)
        return out[::-1]

    def unit_z(i):
        t = z + ((i + 1) // 2) * (1 - 2 * (i % 2))
        return jnp.where(t < 0, t + Z, jnp.where(t >= Z, t - Z, t))

    def column(i):
        return (blk, unit_z(i) * 2 + xhi)

    def seen_from(i):
        return i if i in (0, Z - 1) else (i + 1 if i % 2 else i - 1)

    def unit_of(flips):
        return sum(flip(bit, by) * (1 << b) for b, (bit, by) in enumerate(zip(ubits, flips)))

    def unit_u(j):
        return unit_of(bits_of(j, UB))

    def plane(i, b=None):
        if b is None:
            b, i = i % 4, i // 4
        u = unit_of([b // 2] + bits_of(i, UB - 1))
        return (u * 2 + core, z * 2 + flip(xhi, b % 2))

    def remote(src, dst, ssem, rsem, dev):
        return pltpu.make_async_remote_copy(
            src_ref=src, dst_ref=dst, send_sem=ssem, recv_sem=rsem, device_id=dev, device_id_type=MESH
        )

    def each(low, high, body):
        def step(i, c):
            body(i)
            return c

        lax.fori_loop(low, high, step, 0)

    barrier = pltpu.get_barrier_semaphore()

    def greet(dev):
        pl.semaphore_signal(barrier, inc=1, device_id=dev, device_id_type=MESH)

    greet(sib_dev)
    for i in range(1, Z):
        greet(column(i))
    for i in range(1, PL):
        greet(plane(i))
        greet((unit_u(i // 2) * 2 + xhi, z * 2 + flip(xhi, i % 2)))

    own_copies = [
        pltpu.make_async_copy(series.at[pl.ds(k * PT, PT)], r.xbuf.at[pl.ds(k * PART, PT)], r.x_sem.at[k])
        for k in (0, 1)
    ]
    for copy in own_copies:
        copy.start()
    key_float = positives[...].astype(F32)
    key_norm = jnp.sqrt(jnp.sum(key_float * key_float, axis=1, keepdims=True) + EPSILON)
    r.kbuf[0:TB, :] = (key_float / key_norm).astype(BF16)
    r.prbuf[0] = pair[...]

    pl.semaphore_wait(barrier, 1 + (Z - 1) + (PL - 1) + PL - 2 * jnp.where(holder, 1, 0))

    class Ring:
        def __init__(self, name, buf, base, rows, chunks, source):
            self.buf, self.base, self.rows, self.chunks, self.source = buf, base, rows, chunks, source
            self.sems = [getattr(r, name + s) for s in ("_send", "_recv", "s_send", "s_recv")]

        def place(self, direction, hop):
            return 0 if hop == 0 else min(2 * hop - 1 + direction, Z - 1)

        def chunk_list(self, direction, hop):
            half = self.chunks // 2
            if hop == HOPS:
                return list(range(half)) if direction == 0 else list(range(half, self.chunks))
            order = list(range(self.chunks))
            return order if direction == 0 else order[half:] + order[:half]

        def at(self, i, rel, chunk, count=1):
            size = self.rows // self.chunks
            return self.buf.at[pl.ds(self.base + (i * 2 + rel) * self.rows + chunk * size, size * count)]

        def send(self, direction, hop, chunk):
            size = self.rows // self.chunks
            src = self.at(self.place(direction, hop), 0, chunk)
            if hop == 0 and self.source is not None:
                src = self.source.at[pl.ds(chunk * size, size)]
            k = hop * self.chunks + chunk
            return remote(
                src,
                self.at(self.place(direction, hop + 1), 0, chunk),
                self.sems[0].at[direction, k],
                self.sems[1].at[direction, k],
                column(1 + (1 - direction)),
            )

        def arrival(self, direction, hop, chunk):
            ref = self.at(self.place(direction, hop), 0, chunk)
            k = (hop - 1) * self.chunks + chunk
            return remote(ref, ref, self.sems[0].at[direction, k], self.sems[1].at[direction, k], sib_dev)

        def over(self, direction, hop, chunk, rel=0):
            i = self.place(direction, hop)
            k = (hop - 1) * self.chunks + chunk
            src = self.at(i, rel, chunk)
            return remote(
                src, self.at(i, 1, chunk), self.sems[2].at[direction, k], self.sems[3].at[direction, k], sib_dev
            )

        def over_own(self, rel=0):
            src = self.at(0, rel, 0, self.chunks)
            if rel == 0 and self.source is not None:
                src = self.source
            last = HOPS * self.chunks - self.chunks // 2 - 1 + self.chunks
            return remote(
                src, self.at(0, 1, 0, self.chunks), self.sems[2].at[0, last], self.sems[3].at[0, last], sib_dev
            )

        def begin(self):
            for a, b in zip(self.chunk_list(0, 0), self.chunk_list(1, 0)):
                self.send(0, 0, a).start()
                self.send(1, 0, b).start()
            self.over_own().start()

        def passing(self, hop, n):
            for direction in (0, 1):
                chunk = self.chunk_list(direction, hop)[n]
                self.arrival(direction, hop, chunk).wait_recv()
                if hop + 1 <= HOPS and chunk in self.chunk_list(direction, hop + 1):
                    self.send(direction, hop, chunk).start()
                self.over(direction, hop, chunk).start()

        def passing_all(self, hop):
            for n in range(len(self.chunk_list(0, hop))):
                self.passing(hop, n)

        def other_ready(self, hop):
            for direction in (0, 1) if hop else ():
                for chunk in self.chunk_list(direction, hop):
                    self.over(direction, hop, chunk, 1).wait_recv()
            if hop == 0:
                self.over_own(1).wait_recv()

        def drain(self):
            for direction in (0, 1):
                for hop in range(HOPS + 1):
                    for chunk in self.chunk_list(direction, hop):
                        if hop < HOPS and chunk in self.chunk_list(direction, hop + 1):
                            self.send(direction, hop, chunk).wait_send()
                        if hop:
                            self.over(direction, hop, chunk).wait_send()
            self.over_own().wait_send()

    keys_ring = Ring("k", r.kbuf, 0, TB, KEY_CHUNKS, None)
    rings = [
        Ring("ab"[k], r.xbuf, k * PART, PT, CHUNKS[k], series.at[pl.ds(k * PT, PT)]) for k in (0, 1)
    ]
    keys_ring.begin()
    rings[0].begin()

    partner = (blk, z * 2 + 1 - xhi)
    w_copies = [
        remote(w_last, r.wbuf, r.w_send.at[0], r.w_recv.at[0], partner),
        remote(w_head, r.whbuf, r.w_send.at[1], r.w_recv.at[1], partner),
    ]

    @pl.when(holder)
    def _():
        for copy in w_copies:
            copy.start()
        pltpu.make_async_copy(w_last, r.wbuf, r.w_recv.at[0]).start()
        pltpu.make_async_copy(w_head, r.whbuf, r.w_recv.at[1]).start()

    def pair_copy(j):
        return remote(pair, r.prbuf.at[j], r.pr_send.at[j], r.pr_recv.at[j], plane(j * 2))

    for j in range(1, U):
        pair_copy(j).start()

    class Swap:
        def __init__(self, name, src, dst, part):
            self.src, self.dst = src.at[part], dst.at[part]
            self.ssem, self.rsem = (getattr(r, name + s).at[part] for s in ("_send", "_recv"))

        def copy(self, i, b=None):
            k = i if b is None else i * 4 + b
            return remote(self.src.at[k], self.dst.at[k], self.ssem.at[k], self.rsem.at[k], plane(i, b))

        def own_copy(self, i, b=None):
            k = i if b is None else i * 4 + b
            return remote(self.src.at[0], self.dst.at[k], self.ssem.at[k], self.rsem.at[k], plane(i, b))

    swap_m = [Swap("m", r.msend, r.mrecv, k) for k in (0, 1)]
    swap_q = [Swap("q", r.qbuf, r.qbuf, k) for k in (0, 1)]
    swap_p = [Swap("p", r.psend, r.precv, k) for k in (0, 1)]
    swap_t = [Swap("t", r.tsend, r.trecv, k) for k in (0, 1)]

    def quad(u, body):
        for b in range(4):
            if b == 0:
                pl.when(u != 0)(functools.partial(body, u, b))
            else:
                body(u, b)

    def find_pairs(k):
        def unit(u):
            lanes = lax.broadcasted_iota(jnp.int32, (QUAD, TB), 1)
            cols = []
            for b in range(4):
                row = r.prbuf[u * 2 + b // 2, pl.ds(z * 2 + flip(xhi, b % 2), 1), :]
                cols.append(jnp.broadcast_to(row, (TB, TB)).T[k * PT : (k + 1) * PT, :])
            both = jnp.concatenate(cols, axis=0) - lanes
            total = jnp.zeros((QUAD, E), F32)
            for i in range(Z):
                low = (unit_z(i) * 2 + xhi) * TB
                hot = jnp.concatenate([both == blk * GRP_ROWS + low, both == sib_blk * GRP_ROWS + low], axis=1)
                hot = jnp.where(hot, 1.0, 0.0).astype(BF16)
                total = total + dot_nn(hot, r.kbuf[i * 2 * TB : (i + 1) * 2 * TB, :])
            for b in range(4):
                r.msend[k, u * 4 + b] = total[b * PT : (b + 1) * PT, :].astype(BF16)
            quad(u, lambda *at: swap_m[k].copy(*at).start())

        each(0, PL // 4, unit)

    def block(hop):
        return (0, 1) if hop == 0 else (2 * hop - 1, min(2 * hop + 1, Z))

    def hs_copy(k, i):
        return remote(r.hsend.at[k, i], r.hsib.at[k, i], r.hs_send.at[k, i], r.hs_recv.at[k, i], sib_dev)

    def hd_copy(k, i):
        slot = seen_from(i)
        return remote(r.hdir.at[k, i], r.hrecv.at[k, slot], r.hd_send.at[k, i], r.hd_recv.at[k, slot], column(i))

    def encode(k, hop):
        rings[k].other_ready(hop)
        low, high = block(hop)
        start, stop = k * PART + low * 2 * PT, k * PART + high * 2 * PT
        x = dot_nn(r.xbuf[start:stop, :], r.wbuf[...])
        x2 = x * x
        t = jnp.tanh(GELU_A * (x + GELU_B * (x2 * x)))
        cdf = 0.5 + 0.5 * t
        hidden = x * cdf
        out = dot_nn(hidden.astype(BF16), r.whbuf[...])
        for i in range(low, high):
            first = (i - low) * 2 * PT
            r.hown[k, i] = out[first : first + PT, :]
            r.hsend[k, i] = out[first + PT : first + 2 * PT, :]
            hs_copy(k, i).start()
        r.hidt[:, start:stop] = hidden.T.astype(BF16)
        dgelu = cdf + (0.5 * GELU_A) * x * (1.0 - t * t) * (1.0 + (3.0 * GELU_B) * x2)
        r.dgt[:, start:stop] = dgelu.T

    def head_send(k, hop):
        for i in range(*block(hop)):
            if i:
                hs_copy(k, i).wait_recv()
                r.hdir[k, i] = (r.hown[k, i] + r.hsib[k, i]).astype(BF16)
                hd_copy(k, i).start()

    def make_queries(k):
        hs_copy(k, 0).wait_recv()
        head = r.hown[k, 0] + r.hsib[k, 0]
        for i in range(1, Z):
            hd_copy(k, seen_from(i)).wait_recv()
            head = head + r.hrecv[k, i].astype(F32)
        row_norm = jnp.sqrt(jnp.sum(head * head, axis=1, keepdims=True) + EPSILON)
        unit_rows = head / row_norm
        r.ubuf[k] = unit_rows
        r.rnbuf[k] = jnp.broadcast_to(row_norm, (PT, 128))
        r.qbuf[k, 0] = unit_rows.astype(BF16)
        for i in range(1, PL):
            swap_q[k].own_copy(i).start()

    CHUNK = min(512, KEYS)
    scale = (1.0 / TEMP) * math.log2(math.e)

    def attend(k):
        def unit(u):
            quad(u, lambda *at: swap_q[k].own_copy(*at).wait_recv())
            q = r.qbuf[k, pl.ds(u * 4, 4)].reshape(QUAD, E)
            total = jnp.zeros((QUAD, 128), F32)
            weighted = jnp.zeros((QUAD, E), F32)
            for c in range(KEYS // CHUNK):
                keys = r.kbuf[c * CHUNK : (c + 1) * CHUNK, :]
                e = jnp.exp2(dot_nt(q, keys) * scale)
                total = total + fold_lanes(e)
                weighted = weighted + dot_nn(e.astype(BF16), keys)
            for b in range(4):
                r.psend[k, u * 4 + b] = weighted[b * PT : (b + 1) * PT, :].astype(BF16)
            for b in (0, 1):
                part = jnp.sum(total[b * 2 * PT : (b + 1) * 2 * PT, :].T, axis=0, keepdims=True)
                part = jnp.broadcast_to(part, (8, 2 * PT))
                r.tsend[k, u * 4 + b * 2] = part
                r.tsend[k, u * 4 + b * 2 + 1] = part
            quad(u, lambda *at: swap_p[k].copy(*at).start())
            quad(u, lambda *at: swap_t[k].copy(*at).start())

        each(0, PL // 4, unit)

    def g_rows(k, i, rel):
        return r.gbuf.at[pl.ds(k * PART + (i * 2 + rel) * PT, PT)]

    def g_direct(k, i):
        slot = seen_from(i)
        return remote(g_rows(k, 0, 0), g_rows(k, slot, 0), r.gd_send.at[k, i], r.gd_recv.at[k, slot], column(i))

    def g_arrival(k, i):
        ref = g_rows(k, i, 0)
        return remote(ref, ref, r.gd_send.at[k, i], r.gd_recv.at[k, i], sib_dev)

    def g_over(k, i, rel=0):
        return remote(g_rows(k, i, rel), g_rows(k, i, 1), r.gs_send.at[k, i], r.gs_recv.at[k, i], sib_dev)

    def make_rows(k):
        matched = r.msend[k, 0].astype(F32)
        for i in range(1, PL):
            swap_m[k].copy(i).wait_recv()
            matched = matched + r.mrecv[k, i].astype(F32)
        weighted = r.psend[k, 0].astype(F32)
        totals = [r.tsend[k, 0], jnp.zeros((8, 2 * PT), F32)]
        for i in range(1, PL):
            swap_p[k].copy(i).wait_recv()
            swap_t[k].copy(i).wait_recv()
            weighted = weighted + r.precv[k, i].astype(F32)
            totals[i % 2] = totals[i % 2] + r.trecv[k, i]
        sides = [jnp.broadcast_to(totals[b][0:1, :], (128, 2 * PT)).T for b in (0, 1)]
        total = sides[0][0:PT, :] + sides[1][PT : 2 * PT, :]
        wide = jnp.concatenate([total] * (E // 128), axis=1)
        grad = (weighted / wide - matched) * (1.0 / TEMP)
        unit_rows = r.ubuf[k]
        along = jnp.sum(unit_rows * grad, axis=1, keepdims=True)
        norm = jnp.concatenate([r.rnbuf[k]] * (E // 128), axis=1)
        r.gbuf[k * PART : k * PART + PT, :] = ((grad - unit_rows * along) / norm).astype(BF16)
        g_over(k, 0).start()
        for i in range(1, Z):
            g_direct(k, i).start()
        hit = r.qbuf[k, 0].astype(F32) * matched
        hit = fold_lanes(jnp.sum(hit.reshape(PT // 8, 8, E), axis=0))
        logs = jnp.sum(jnp.log(total).reshape(PT // 8, 8, 128), axis=0)
        first = lax.broadcasted_iota(jnp.int32, (8, 128), 1) == 0
        return jnp.where(first, logs, 0.0) - hit * (1.0 / TEMP)

    def back(k):
        for hop in range(HOPS + 1):
            low, high = block(hop)
            for i in range(low, high):
                if i:
                    g_arrival(k, i).wait_recv()
                    g_over(k, i).start()
            for i in range(low, high):
                g_over(k, i, 1).wait_recv()
            start, stop = k * PART + low * 2 * PT, k * PART + high * 2 * PT
            dp = dot_nt(r.whbuf[...], r.gbuf[start:stop, :]) * r.dgt[:, start:stop]
            r.dpt[:, start:stop] = dp.astype(BF16)

    def lp_copy(i):
        return remote(r.lplane.at[pid], r.lplane.at[pid], r.lp_send.at[i], r.lp_recv.at[i], plane(i))

    def lp_arrival(i):
        p = unit_u(i // 2) * 2 + flip(xhi, i % 2)
        return remote(r.lplane.at[p], r.lplane.at[p], r.lp_send.at[i], r.lp_recv.at[i], sib_dev)

    def lc_copy(i):
        ref = r.lcol.at[z]
        return remote(ref, ref, r.lc_send.at[i], r.lc_recv.at[seen_from(i)], column(i))

    def lc_arrival(i):
        ref = r.lcol.at[unit_z(i)]
        return remote(ref, ref, r.lc_send.at[i], r.lc_recv.at[i], sib_dev)

    def ls_copy(c):
        return remote(r.lsib.at[c], r.lsib.at[c], r.ls_send, r.ls_recv, sib_dev)

    for copy in own_copies:
        copy.wait()
    for hop in range(1, HOPS):
        keys_ring.passing_all(hop)
        rings[0].passing_all(hop)
    rings[1].begin()
    for copy in w_copies:
        copy.wait_recv()
    for hop in range(HOPS - 1):
        encode(0, hop)
    for j in range(1, U):
        pair_copy(j).wait_recv()
    keys_ring.passing_all(HOPS)
    rings[0].passing_all(HOPS)
    encode(0, HOPS - 1)
    encode(0, HOPS)
    for hop in range(1, HOPS - 1):
        head_send(0, hop)
    rings[1].passing(1, 0)
    head_send(0, HOPS - 1)
    head_send(0, HOPS)
    for n in range(1, CHUNKS[1]):
        rings[1].passing(1, n)
    for hop in range(HOPS + 1):
        keys_ring.other_ready(hop)
    find_pairs(0)
    rings[1].passing_all(2)
    make_queries(0)
    find_pairs(1)
    rings[1].passing_all(3)
    encode(1, 0)
    attend(0)
    encode(1, 1)
    rings[1].passing_all(4)
    encode(1, 2)
    encode(1, 3)
    encode(1, 4)
    for hop in range(1, HOPS + 1):
        head_send(1, hop)
    loss = make_rows(0)
    make_queries(1)
    back(0)
    attend(1)
    loss = loss + make_rows(1)
    r.lplane[pid] = loss
    for i in range(1, PL):
        lp_copy(i).start()
    back(1)

    ghead = dot_nn(r.hidt[...], r.gbuf[...])
    r.ghb[...] = ghead.T.astype(BF16)

    for i in range(1, PL):
        lp_arrival(i).wait_recv()
    loss = r.lplane[0]
    for p in range(1, PL):
        loss = loss + r.lplane[p]
    r.lcol[z] = loss
    for i in range(1, Z):
        lc_copy(i).start()

    def f_copy(j, c):
        slot = j * 2 + jnp.where(holder, 0, 1)
        return remote(
            r.fsend.at[j, c],
            r.frecv.at[slot],
            r.f_send.at[j, c],
            r.f_recv.at[slot],
            (unit_u(j) * 2 + c, z * 2 + core),
        )

    def f_local(j, c):
        return jnp.logical_and(jnp.logical_and(holder, j == 0), c == core)

    def last(step):
        j = U - 1 - step
        n = unit_u(j)
        cols = pl.ds(pl.multiple_of(n * 2 * DS, 2 * DS), 2 * DS)
        part = dot_nn(r.dpt[...], r.xbuf[:, cols]).astype(BF16)
        for c in (0, 1):
            d = n * 2 + c
            r.fsend[j, c, 0:HS, :] = part[:, c * DS : (c + 1) * DS]
            gh = r.ghb[pl.ds(pl.multiple_of(d * ES, 16), ES), :]
            for w in range(HS // 128):
                r.fsend[j, c, HS + w * ES : HS + (w + 1) * ES, :] = gh[:, w * 128 : (w + 1) * 128]

            @pl.when(jnp.logical_not(f_local(j, c)))
            def _():
                f_copy(j, c).start()

            @pl.when(f_local(j, c))
            def _():
                pltpu.make_async_copy(r.fsend.at[j, c], r.frecv.at[0], r.f_recv.at[0]).start()

    each(0, U, last)

    for i in range(1, Z):
        lc_arrival(i).wait_recv()
    loss = r.lcol[0]
    for p in range(1, Z):
        loss = loss + r.lcol[p]
    r.lsib[core] = loss
    ls_copy(core).start()

    for ring in [keys_ring] + rings:
        ring.drain()

    @pl.when(holder)
    def _():
        for copy in w_copies:
            copy.wait_send()

    for j in range(1, U):
        pair_copy(j).wait_send()
    for k in (0, 1):
        for i in range(Z):
            hs_copy(k, i).wait_send()
            g_over(k, i).wait_send()
            if i:
                hd_copy(k, i).wait_send()
                g_direct(k, i).wait_send()
        for i in range(1, PL):
            swap_q[k].own_copy(i).wait_send()
            swap_m[k].copy(i).wait_send()
            swap_p[k].copy(i).wait_send()
            swap_t[k].copy(i).wait_send()
    for i in range(1, PL):
        lp_copy(i).wait_send()
    for i in range(1, Z):
        lc_copy(i).wait_send()

    ls_copy(1 - core).wait_recv()
    ls_copy(core).wait_send()
    loss = r.lsib[0] + r.lsib[1]
    loss = jnp.sum(loss, axis=1, keepdims=True)
    loss_out[...] = jnp.sum(loss, axis=0, keepdims=True) * (1.0 / TOKENS)

    def f_arrival(s):
        return remote(r.frecv.at[s], r.frecv.at[s], r.f_send.at[0, 0], r.f_recv.at[s], sib_dev)

    each(0, PL, lambda s: f_arrival(s).wait_recv())
    total = r.frecv[0].astype(F32)
    for s in range(1, PL):
        total = total + r.frecv[s].astype(F32)
    gl_out[...] = total[0:HS, :].T
    for w in range(HS // 128):
        gh_out[:, w * 128 : (w + 1) * 128] = total[HS + w * ES : HS + (w + 1) * ES, :]

    def f_sent(j):
        for c in (0, 1):

            @pl.when(jnp.logical_not(f_local(j, c)))
            def _():
                f_copy(j, c).wait_send()

    each(0, U, f_sent)


def solution(mesh):
    PL = mesh.shape["blk"]
    Z = mesh.shape["grp"] // 2
    M = 2 * Z

    def on_device(series, positives, w_last, w_head, pair_index):
        TB, D = series.shape
        HS = w_last.shape[1]
        E = w_head.shape[1]
        PT = TB // 2
        DS, ES = D // PL, E // PL
        dims = (Z, PL, TB, D, HS, E, TB * PL * M)
        pair = pair_index.reshape(M, TB)
        vm, sem = pltpu.VMEM, pltpu.SemaphoreType.DMA
        rows = M * TB
        fr = HS + ES * (HS // 128)
        scratch = dict(
            xbuf=vm((rows, D), BF16),
            wbuf=vm((D, HS), BF16),
            whbuf=vm((HS, E), BF16),
            kbuf=vm((rows, E), BF16),
            prbuf=vm((PL // 2, M, TB), jnp.int32),
            msend=vm((2, PL, PT, E), BF16),
            mrecv=vm((2, PL, PT, E), BF16),
            hidt=vm((HS, rows), BF16),
            dgt=vm((HS, rows), F32),
            hown=vm((2, Z, PT, E), F32),
            hsend=vm((2, Z, PT, E), F32),
            hsib=vm((2, Z, PT, E), F32),
            hdir=vm((2, Z, PT, E), BF16),
            hrecv=vm((2, Z, PT, E), BF16),
            ubuf=vm((2, PT, E), F32),
            rnbuf=vm((2, PT, 128), F32),
            qbuf=vm((2, PL, PT, E), BF16),
            psend=vm((2, PL, PT, E), BF16),
            precv=vm((2, PL, PT, E), BF16),
            tsend=vm((2, PL, 8, 2 * PT), F32),
            trecv=vm((2, PL, 8, 2 * PT), F32),
            gbuf=vm((rows, E), BF16),
            dpt=vm((HS, rows), BF16),
            ghb=vm((E, HS), BF16),
            fsend=vm((PL // 2, 2, fr, DS), BF16),
            frecv=vm((PL, fr, DS), BF16),
            lplane=vm((PL, 8, 128), F32),
            lcol=vm((Z, 8, 128), F32),
            lsib=vm((2, 8, 128), F32),
            x_sem=sem((2,)),
            ls_send=sem,
            ls_recv=sem,
        )
        hops = Z // 2
        sems = dict(
            w=(2,), pr=(PL // 2,), m=(2, PL), hs=(2, Z), hd=(2, Z), q=(2, PL), p=(2, PL), t=(2, PL),
            gd=(2, Z), gs=(2, Z), lp=(PL,), lc=(Z,), f=(PL // 2, 2),
        )
        for name, chunks in (("k", KEY_CHUNKS), ("a", CHUNKS[0]), ("b", CHUNKS[1])):
            sems[name] = (2, hops * chunks)
            sems[name + "s"] = (2, hops * chunks + chunks // 2)
        for name, shape in sems.items():
            scratch[name + "_send"] = sem(shape)
            scratch[name + "_recv"] = sem((PL,) if name == "f" else shape)
        names = list(scratch)

        def body(*refs):
            kernel(dims, refs[:5], refs[5:8], types.SimpleNamespace(**dict(zip(names, refs[8:]))))

        any_spec = pl.BlockSpec(memory_space=pl.ANY)
        vm_spec = pl.BlockSpec(memory_space=pltpu.VMEM)
        loss, grad_last, grad_head = pl.pallas_call(
            body,
            out_shape=(
                jax.ShapeDtypeStruct((1, 1), F32),
                jax.ShapeDtypeStruct((DS, HS), F32),
                jax.ShapeDtypeStruct((ES, HS), F32),
            ),
            in_specs=[any_spec, vm_spec, any_spec, any_spec, vm_spec],
            out_specs=(vm_spec, vm_spec, vm_spec),
            scratch_shapes=list(scratch.values()),
            compiler_params=pltpu.CompilerParams(
                collective_id=0, has_side_effects=True, vmem_limit_bytes=VMEM_BYTES
            ),
        )(series, positives, w_last, w_head, pair)
        return (loss[0, 0], grad_last, grad_head.T)

    return jax.shard_map(
        on_device,
        mesh=mesh,
        in_specs=(
            P(("blk", "grp"), None),
            P(("blk", "grp"), None),
            P(None, "grp"),
            P("grp", None),
            P("blk"),
        ),
        out_specs=(P(), P("blk", "grp"), P("grp", "blk")),
        check_vma=False,
    )
```

```python
import functools
import math
import types

import jax
import jax.numpy as jnp
from jax import lax
from jax.experimental import pallas as pl
from jax.experimental.pallas import tpu as pltpu
from jax.sharding import PartitionSpec as P

MESH = pl.DeviceIdType.MESH
F32 = jnp.float32
BF16 = jnp.bfloat16

TEMP = 0.05
EPSILON = 1e-06
GELU_A = math.sqrt(2.0 / math.pi)
GELU_B = 0.044715
KEY_CHUNKS = 2
PARTS = (64, 64)
CHUNKS = (2, 2)
GROUPS = (4, 4)
VMEM_BYTES = 56 * 1024 * 1024


def dot_nn(left, right):
    return lax.dot_general(left, right, (((1,), (0,)), ((), ())), preferred_element_type=F32)


def dot_nt(left, right):
    return lax.dot_general(left, right, (((1,), (1,)), ((), ())), preferred_element_type=F32)


def fold_lanes(x):
    total = x[:, 0:128]
    for k in range(1, x.shape[1] // 128):
        total = total + x[:, k * 128 : (k + 1) * 128]
    return total


def kernel(dims, refs_in, refs_out, refs):
    Z, PL, TB, D, HS, E, TOKENS = dims
    series, positives, w_last, w_head, pair = refs_in
    loss_out, gl_out, gh_out = refs_out
    r = refs
    U = PL // 2
    HOPS = Z // 2
    K = len(PARTS)
    first_row = [sum(PARTS[:k]) for k in range(K)]
    part_row = [2 * Z * f for f in first_row]
    group = GROUPS
    g_bits = [g.bit_length() - 1 for g in group]
    KEYS = 2 * Z * TB
    DS = D // PL
    ES = E // PL
    GRP_ROWS = 2 * Z * TB
    blk = lax.axis_index("blk")
    grp = lax.axis_index("grp")
    core = blk % 2
    xhi = grp % 2
    z = grp // 2
    uid = blk // 2
    pid = uid * 2 + xhi
    sib_blk = uid * 2 + 1 - core
    sib_dev = (sib_blk, grp)
    holder = core == xhi

    UB = U.bit_length() - 1
    ubits = [(uid // (1 << b)) % 2 for b in range(UB)]

    def flip(bit, by):
        if isinstance(by, int):
            return 1 - bit if by else bit
        return bit + by - 2 * bit * by

    def bits_of(j, count):
        if isinstance(j, int):
            return [(j >> b) & 1 for b in range(count)]
        out = []
        for b in reversed(range(count)):
            bit = jnp.where(j >= (1 << b), 1, 0)
            out.append(bit)
            j = j - bit * (1 << b)
        return out[::-1]

    def unit_z(i):
        t = z + ((i + 1) // 2) * (1 - 2 * (i % 2))
        return jnp.where(t < 0, t + Z, jnp.where(t >= Z, t - Z, t))

    def column(i):
        return (blk, unit_z(i) * 2 + xhi)

    def seen_from(i):
        return i if i in (0, Z - 1) else (i + 1 if i % 2 else i - 1)

    def unit_of(flips):
        return sum(flip(bit, by) * (1 << b) for b, (bit, by) in enumerate(zip(ubits, flips)))

    def unit_u(j):
        return unit_of(bits_of(j, UB))

    def plane(i, b=None, low=1):
        if b is None:
            b, i = i % 2, i // 2
        u = unit_of(bits_of(b // 2, low - 1) + bits_of(i, UB + 1 - low))
        return (u * 2 + core, z * 2 + flip(xhi, b % 2))

    def position(i):
        return i - 1 if 0 < i < Z - 1 else (Z - 2 if i == 0 else i)

    def remote(src, dst, ssem, rsem, dev):
        return pltpu.make_async_remote_copy(
            src_ref=src, dst_ref=dst, send_sem=ssem, recv_sem=rsem, device_id=dev, device_id_type=MESH
        )

    def each(low, high, body):
        def step(i, c):
            body(i)
            return c

        lax.fori_loop(low, high, step, 0)

    def parts_of(name):
        return [getattr(r, name + str(k)) for k in range(K)]

    msend, mrecv, qbuf, psend, precv, tsend, trecv = map(
        parts_of, ("msend", "mrecv", "qbuf", "psend", "precv", "tsend", "trecv")
    )
    hown, hsend, hsib, hdir, hrecv, ubuf, rnbuf = map(
        parts_of, ("hown", "hsend", "hsib", "hdir", "hrecv", "ubuf", "rnbuf")
    )

    barrier = pltpu.get_barrier_semaphore()

    def greet(dev):
        pl.semaphore_signal(barrier, inc=1, device_id=dev, device_id_type=MESH)

    greet(sib_dev)
    for i in range(1, Z):
        greet(column(i))
    for i in range(1, PL):
        greet(plane(i))
        greet((unit_u(i // 2) * 2 + xhi, z * 2 + flip(xhi, i % 2)))

    own_copies = [
        pltpu.make_async_copy(
            series.at[pl.ds(first_row[k], PARTS[k])],
            r.xbuf.at[pl.ds(part_row[k] + position(0) * 2 * PARTS[k], PARTS[k])],
            r.x_sem.at[k],
        )
        for k in range(K)
    ]
    for copy in own_copies:
        copy.start()
    key_float = positives[...].astype(F32)
    key_norm = jnp.sqrt(jnp.sum(key_float * key_float, axis=1, keepdims=True) + EPSILON)
    r.kbuf[position(0) * 2 * TB : position(0) * 2 * TB + TB, :] = (key_float / key_norm).astype(BF16)
    r.prbuf[0] = pair[...]

    pl.semaphore_wait(barrier, 1 + (Z - 1) + (PL - 1) + PL - 2 * jnp.where(holder, 1, 0))

    class Ring:
        def __init__(self, name, buf, base, rows, chunks, source):
            self.buf, self.base, self.rows, self.chunks, self.source = buf, base, rows, chunks, source
            self.sems = [getattr(r, name + s) for s in ("_send", "_recv", "s_send", "s_recv")]

        def place(self, direction, hop):
            return 0 if hop == 0 else min(2 * hop - 1 + direction, Z - 1)

        def chunk_list(self, direction, hop):
            half = self.chunks // 2
            if hop == HOPS:
                return list(range(half)) if direction == 0 else list(range(half, self.chunks))
            order = list(range(self.chunks))
            return order if direction == 0 else order[half:] + order[:half]

        def at(self, i, rel, chunk, count=1):
            size = self.rows // self.chunks
            return self.buf.at[pl.ds(self.base + (position(i) * 2 + rel) * self.rows + chunk * size, size * count)]

        def send(self, direction, hop, chunk):
            size = self.rows // self.chunks
            src = self.at(self.place(direction, hop), 0, chunk)
            if hop == 0 and self.source is not None:
                src = self.source.at[pl.ds(chunk * size, size)]
            k = hop * self.chunks + chunk
            return remote(
                src,
                self.at(self.place(direction, hop + 1), 0, chunk),
                self.sems[0].at[direction, k],
                self.sems[1].at[direction, k],
                column(1 + (1 - direction)),
            )

        def arrival(self, direction, hop, chunk):
            ref = self.at(self.place(direction, hop), 0, chunk)
            k = (hop - 1) * self.chunks + chunk
            return remote(ref, ref, self.sems[0].at[direction, k], self.sems[1].at[direction, k], sib_dev)

        def over(self, direction, hop, chunk, rel=0):
            i = self.place(direction, hop)
            k = (hop - 1) * self.chunks + chunk
            src = self.at(i, rel, chunk)
            return remote(
                src, self.at(i, 1, chunk), self.sems[2].at[direction, k], self.sems[3].at[direction, k], sib_dev
            )

        def over_own(self, rel=0):
            src = self.at(0, rel, 0, self.chunks)
            if rel == 0 and self.source is not None:
                src = self.source
            last = HOPS * self.chunks - self.chunks // 2 - 1 + self.chunks
            return remote(
                src, self.at(0, 1, 0, self.chunks), self.sems[2].at[0, last], self.sems[3].at[0, last], sib_dev
            )

        def begin_with(self, n):
            for direction in (0, 1):
                self.send(direction, 0, self.chunk_list(direction, 0)[n]).start()

        def begin(self):
            for n in range(self.chunks):
                self.begin_with(n)
            self.over_own().start()

        def passing(self, hop, n):
            for direction in (0, 1):
                chunk = self.chunk_list(direction, hop)[n]
                self.arrival(direction, hop, chunk).wait_recv()
                if hop + 1 <= HOPS and chunk in self.chunk_list(direction, hop + 1):
                    self.send(direction, hop, chunk).start()
                self.over(direction, hop, chunk).start()

        def passing_all(self, hop):
            for n in range(len(self.chunk_list(0, hop))):
                self.passing(hop, n)

        def other_ready(self, hop):
            for direction in (0, 1) if hop else ():
                for chunk in self.chunk_list(direction, hop):
                    self.over(direction, hop, chunk, 1).wait_recv()
            if hop == 0:
                self.over_own(1).wait_recv()

        def drain(self):
            for direction in (0, 1):
                for hop in range(HOPS + 1):
                    for chunk in self.chunk_list(direction, hop):
                        if hop < HOPS and chunk in self.chunk_list(direction, hop + 1):
                            self.send(direction, hop, chunk).wait_send()
                        if hop:
                            self.over(direction, hop, chunk).wait_send()
            self.over_own().wait_send()

    keys_ring = Ring("k", r.kbuf, 0, TB, KEY_CHUNKS, None)
    rings = [
        Ring("x%d" % k, r.xbuf, part_row[k], PARTS[k], CHUNKS[k], series.at[pl.ds(first_row[k], PARTS[k])])
        for k in range(K)
    ]
    keys_ring.begin()
    rings[0].begin_with(0)

    partner = (blk, z * 2 + 1 - xhi)
    w_copies = [
        remote(w_last, r.wbuf, r.w_send.at[0], r.w_recv.at[0], partner),
        remote(w_head, r.whbuf, r.w_send.at[1], r.w_recv.at[1], partner),
    ]

    @pl.when(holder)
    def _():
        for copy in w_copies:
            copy.start()
        pltpu.make_async_copy(w_last, r.wbuf, r.w_recv.at[0]).start()
        pltpu.make_async_copy(w_head, r.whbuf, r.w_recv.at[1]).start()

    def pair_copy(j):
        return remote(pair, r.prbuf.at[j], r.pr_send.at[j], r.pr_recv.at[j], plane(j * 2))

    for j in range(1, U):
        pair_copy(j).start()

    class Swap:
        def __init__(self, name, src, dst, k):
            self.src, self.dst, self.k = getattr(r, src + str(k)), getattr(r, dst + str(k)), k
            self.ssem, self.rsem = (getattr(r, name + s).at[k] for s in ("_send", "_recv"))

        def copy(self, i, b=None, own=False):
            k = i if b is None else i * group[self.k] + b
            dev = plane(i) if b is None else plane(i, b, g_bits[self.k])
            src = self.src.at[0 if own else k]
            return remote(src, self.dst.at[k], self.ssem.at[k], self.rsem.at[k], dev)

        def own_copy(self, i, b=None):
            return self.copy(i, b, True)

    swap_m = [Swap("m", "msend", "mrecv", k) for k in range(K)]
    swap_q = [Swap("q", "qbuf", "qbuf", k) for k in range(K)]
    swap_p = [Swap("p", "psend", "precv", k) for k in range(K)]
    swap_t = [Swap("t", "tsend", "trecv", k) for k in range(K)]

    def members(k, u, body):
        for b in range(group[k]):
            if b == 0:
                pl.when(u != 0)(functools.partial(body, u, b))
            else:
                body(u, b)

    def find_pairs(k, low, high):
        n, g = PARTS[k], group[k]
        UNIT = n * g

        def unit(u):
            lanes = lax.broadcasted_iota(jnp.int32, (UNIT, TB), 1)
            cols = []
            for b in range(g):
                row = r.prbuf[u * (g // 2) + b // 2, pl.ds(z * 2 + flip(xhi, b % 2), 1), :]
                cols.append(jnp.broadcast_to(row, (TB, TB)).T[first_row[k] : first_row[k] + n, :])
            both = jnp.concatenate(cols, axis=0) - lanes
            total = jnp.zeros((UNIT, E), F32)
            for i in range(Z):
                base = (unit_z(i) * 2 + xhi) * TB
                hot = jnp.concatenate([both == blk * GRP_ROWS + base, both == sib_blk * GRP_ROWS + base], axis=1)
                hot = jnp.where(hot, 1.0, 0.0).astype(BF16)
                at = position(i) * 2 * TB
                total = total + dot_nn(hot, r.kbuf[at : at + 2 * TB, :])
            for b in range(g):
                msend[k][u * g + b] = total[b * n : (b + 1) * n, :].astype(BF16)
            members(k, u, lambda *at: swap_m[k].copy(*at).start())

        each(low, high, unit)

    def places(hops):
        out = []
        for hop in hops:
            out += [0] if hop == 0 else ([Z - 1] if hop == HOPS else [2 * hop - 1, 2 * hop])
        return out

    def span(k, hops):
        at = [position(i) for i in places(hops)]
        return part_row[k] + at[0] * 2 * PARTS[k], part_row[k] + (at[-1] + 1) * 2 * PARTS[k]

    def hs_copy(k, i):
        return remote(hsend[k].at[i], hsib[k].at[i], r.hs_send.at[k, i], r.hs_recv.at[k, i], sib_dev)

    def hd_copy(k, i):
        slot = seen_from(i)
        return remote(hdir[k].at[i], hrecv[k].at[slot], r.hd_send.at[k, i], r.hd_recv.at[k, slot], column(i))

    def encode(k, *hops):
        n = PARTS[k]
        for hop in hops:
            rings[k].other_ready(hop)
        start, stop = span(k, hops)
        x = dot_nn(r.xbuf[start:stop, :], r.wbuf[...])
        x2 = x * x
        t = jnp.tanh(GELU_A * (x + GELU_B * (x2 * x)))
        cdf = 0.5 + 0.5 * t
        hidden = x * cdf
        out = dot_nn(hidden.astype(BF16), r.whbuf[...])
        for m, i in enumerate(places(hops)):
            hown[k][i] = out[m * 2 * n : m * 2 * n + n, :]
            hsend[k][i] = out[m * 2 * n + n : (m + 1) * 2 * n, :]
            hs_copy(k, i).start()
        r.hidt[:, start:stop] = hidden.T.astype(BF16)
        dgelu = cdf + (0.5 * GELU_A) * x * (1.0 - t * t) * (1.0 + (3.0 * GELU_B) * x2)
        r.dgt[:, start:stop] = dgelu.T

    def head_send(k, *hops):
        for i in places(hops):
            if i:
                hs_copy(k, i).wait_recv()
                hdir[k][i] = (hown[k][i] + hsib[k][i]).astype(BF16)
                hd_copy(k, i).start()

    def make_queries(k):
        hs_copy(k, 0).wait_recv()
        head = hown[k][0] + hsib[k][0]
        for i in range(1, Z):
            hd_copy(k, seen_from(i)).wait_recv()
            head = head + hrecv[k][i].astype(F32)
        row_norm = jnp.sqrt(jnp.sum(head * head, axis=1, keepdims=True) + EPSILON)
        unit_rows = head / row_norm
        ubuf[k][...] = unit_rows
        rnbuf[k][...] = jnp.broadcast_to(row_norm, (PARTS[k], 128))
        qbuf[k][0] = unit_rows.astype(BF16)
        for i in range(1, PL):
            swap_q[k].own_copy(i).start()

    CHUNK = min(512, KEYS)
    scale = (1.0 / TEMP) * math.log2(math.e)

    def attend(k, low, high):
        n, g = PARTS[k], group[k]
        UNIT = n * g

        def unit(u):
            members(k, u, lambda *at: swap_q[k].own_copy(*at).wait_recv())
            q = qbuf[k][pl.ds(u * g, g)].reshape(UNIT, E)
            total = jnp.zeros((UNIT, 128), F32)
            weighted = jnp.zeros((UNIT, E), F32)
            for c in range(KEYS // CHUNK):
                keys = r.kbuf[c * CHUNK : (c + 1) * CHUNK, :]
                e = jnp.exp2(dot_nt(q, keys) * scale)
                total = total + fold_lanes(e)
                weighted = weighted + dot_nn(e.astype(BF16), keys)
            for b in range(g):
                psend[k][u * g + b] = weighted[b * n : (b + 1) * n, :].astype(BF16)
            members(k, u, lambda *at: swap_p[k].copy(*at).start())
            part = jnp.sum(total.T, axis=0, keepdims=True)
            for b in range(g):
                tsend[k][u * g + b] = part
            members(k, u, lambda *at: swap_t[k].copy(*at).start())

        each(low, high, unit)

    def g_rows(k, i, rel):
        return r.gbuf.at[pl.ds(part_row[k] + (position(i) * 2 + rel) * PARTS[k], PARTS[k])]

    def g_direct(k, i):
        slot = seen_from(i)
        return remote(g_rows(k, 0, 0), g_rows(k, slot, 0), r.gd_send.at[k, i], r.gd_recv.at[k, slot], column(i))

    def g_arrival(k, i):
        ref = g_rows(k, i, 0)
        return remote(ref, ref, r.gd_send.at[k, i], r.gd_recv.at[k, i], sib_dev)

    def g_over(k, i, rel=0):
        return remote(g_rows(k, i, rel), g_rows(k, i, 1), r.gs_send.at[k, i], r.gs_recv.at[k, i], sib_dev)

    def make_rows(k):
        n, g = PARTS[k], group[k]
        UNIT = n * g
        matched = msend[k][0].astype(F32)
        for i in range(1, PL):
            swap_m[k].copy(i).wait_recv()
            matched = matched + mrecv[k][i].astype(F32)
        weighted = psend[k][0].astype(F32)
        lanes = lax.broadcasted_iota(jnp.int32, (1, UNIT), 1)
        side = [jnp.logical_and(lanes >= b * n, lanes < (b + 1) * n) for b in range(g)]
        totals = jnp.where(side[0], tsend[k][0], 0.0)
        for i in range(1, PL):
            swap_p[k].copy(i).wait_recv()
            swap_t[k].copy(i).wait_recv()
            weighted = weighted + precv[k][i].astype(F32)
            totals = totals + jnp.where(side[i % g], trecv[k][i], 0.0)
        column_totals = jnp.broadcast_to(totals, (128, UNIT)).T
        total = column_totals[0:n, :]
        for b in range(1, g):
            total = total + column_totals[b * n : (b + 1) * n, :]
        wide = jnp.concatenate([total] * (E // 128), axis=1)
        grad = (weighted / wide - matched) * (1.0 / TEMP)
        unit_rows = ubuf[k][...]
        along = jnp.sum(unit_rows * grad, axis=1, keepdims=True)
        norm = jnp.concatenate([rnbuf[k][...]] * (E // 128), axis=1)
        g_rows(k, 0, 0)[...] = ((grad - unit_rows * along) / norm).astype(BF16)
        g_over(k, 0).start()
        for i in range(1, Z):
            g_direct(k, i).start()
        hit = qbuf[k][0].astype(F32) * matched
        hit = fold_lanes(jnp.sum(hit.reshape(n // 8, 8, E), axis=0))
        logs = jnp.sum(jnp.log(total).reshape(n // 8, 8, 128), axis=0)
        first = lax.broadcasted_iota(jnp.int32, (8, 128), 1) == 0
        return jnp.where(first, logs, 0.0) - hit * (1.0 / TEMP)

    def back(k, *hops):
        for i in places(hops):
            if i:
                g_arrival(k, i).wait_recv()
                g_over(k, i).start()
        for i in places(hops):
            g_over(k, i, 1).wait_recv()
        start, stop = span(k, hops)
        dp = dot_nt(r.whbuf[...], r.gbuf[start:stop, :]) * r.dgt[:, start:stop]
        r.dpt[:, start:stop] = dp.astype(BF16)

    def lp_copy(i):
        return remote(r.lplane.at[pid], r.lplane.at[pid], r.lp_send.at[i], r.lp_recv.at[i], plane(i))

    def lp_arrival(i):
        p = unit_u(i // 2) * 2 + flip(xhi, i % 2)
        return remote(r.lplane.at[p], r.lplane.at[p], r.lp_send.at[i], r.lp_recv.at[i], sib_dev)

    def lc_copy(i):
        ref = r.lcol.at[z]
        return remote(ref, ref, r.lc_send.at[i], r.lc_recv.at[seen_from(i)], column(i))

    def lc_arrival(i):
        ref = r.lcol.at[unit_z(i)]
        return remote(ref, ref, r.lc_send.at[i], r.lc_recv.at[i], sib_dev)

    def ls_copy(c):
        return remote(r.lsib.at[c], r.lsib.at[c], r.ls_send, r.ls_recv, sib_dev)

    for copy in own_copies:
        copy.wait()
    keys_ring.passing_all(1)
    rings[0].begin_with(1)
    rings[0].over_own().start()
    keys_ring.passing_all(2)
    rings[0].passing(1, 0)
    keys_ring.passing_all(3)
    rings[0].passing(1, 1)
    keys_ring.passing_all(4)
    rings[0].passing(2, 0)
    for j in range(1, U):
        pair_copy(j).wait_recv()
    for hop in range(HOPS + 1):
        keys_ring.other_ready(hop)
    find_pairs(0, 0, 2)
    rings[0].passing(2, 1)
    find_pairs(0, 2, 4)
    rings[0].passing(3, 0)
    find_pairs(1, 0, 2)
    rings[0].passing(3, 1)
    rings[1].begin()
    find_pairs(1, 2, 4)
    for copy in w_copies:
        copy.wait_recv()
    encode(0, 1)
    encode(0, 2)
    rings[0].passing_all(4)
    encode(0, 3)
    head_send(0, 1, 2)
    encode(0, 0, 4)
    head_send(0, 3, 0, 4)
    rings[1].passing_all(1)
    rings[1].passing_all(2)
    encode(1, 1)
    rings[1].passing_all(3)
    encode(1, 2)
    make_queries(0)
    rings[1].passing_all(4)
    encode(1, 3)
    encode(1, 0, 4)
    head_send(1, 1, 2, 3, 0, 4)
    attend(0, 0, 4)
    make_queries(1)
    loss = make_rows(0)
    attend(1, 0, 4)
    back(0, 1, 2)
    back(0, 3, 0, 4)
    loss = loss + make_rows(1)
    r.lplane[pid] = loss
    for i in range(1, PL):
        lp_copy(i).start()
    back(1, 1, 2)
    back(1, 3, 0, 4)

    ghead = dot_nn(r.hidt[...], r.gbuf[...])
    r.ghb[...] = ghead.T.astype(BF16)

    for i in range(1, PL):
        lp_arrival(i).wait_recv()
    loss = r.lplane[0]
    for p in range(1, PL):
        loss = loss + r.lplane[p]
    r.lcol[z] = loss
    for i in range(1, Z):
        lc_copy(i).start()

    def f_copy(j, c):
        slot = j * 2 + jnp.where(holder, 0, 1)
        return remote(
            r.fsend.at[j, c],
            r.frecv.at[slot],
            r.f_send.at[j, c],
            r.f_recv.at[slot],
            (unit_u(j) * 2 + c, z * 2 + core),
        )

    def f_local(j, c):
        return jnp.logical_and(jnp.logical_and(holder, j == 0), c == core)

    def last(step):
        j = U - 1 - step
        n = unit_u(j)
        cols = pl.ds(pl.multiple_of(n * 2 * DS, 2 * DS), 2 * DS)
        part = dot_nn(r.dpt[...], r.xbuf[:, cols]).astype(BF16)
        for c in (0, 1):
            d = n * 2 + c
            r.fsend[j, c, 0:HS, :] = part[:, c * DS : (c + 1) * DS]
            gh = r.ghb[pl.ds(pl.multiple_of(d * ES, 16), ES), :]
            for w in range(HS // 128):
                r.fsend[j, c, HS + w * ES : HS + (w + 1) * ES, :] = gh[:, w * 128 : (w + 1) * 128]

            @pl.when(jnp.logical_not(f_local(j, c)))
            def _():
                f_copy(j, c).start()

            @pl.when(f_local(j, c))
            def _():
                pltpu.make_async_copy(r.fsend.at[j, c], r.frecv.at[0], r.f_recv.at[0]).start()

    each(0, U, last)

    for i in range(1, Z):
        lc_arrival(i).wait_recv()
    loss = r.lcol[0]
    for p in range(1, Z):
        loss = loss + r.lcol[p]
    r.lsib[core] = loss
    ls_copy(core).start()

    for ring in [keys_ring] + rings:
        ring.drain()

    @pl.when(holder)
    def _():
        for copy in w_copies:
            copy.wait_send()

    for j in range(1, U):
        pair_copy(j).wait_send()
    for k in range(K):
        for i in range(Z):
            hs_copy(k, i).wait_send()
            g_over(k, i).wait_send()
            if i:
                hd_copy(k, i).wait_send()
                g_direct(k, i).wait_send()
        for i in range(1, PL):
            swap_q[k].own_copy(i).wait_send()
            swap_m[k].copy(i).wait_send()
            swap_p[k].copy(i).wait_send()
            swap_t[k].copy(i).wait_send()
    for i in range(1, PL):
        lp_copy(i).wait_send()
    for i in range(1, Z):
        lc_copy(i).wait_send()

    ls_copy(1 - core).wait_recv()
    ls_copy(core).wait_send()
    loss = r.lsib[0] + r.lsib[1]
    loss = jnp.sum(loss, axis=1, keepdims=True)
    loss_out[...] = jnp.sum(loss, axis=0, keepdims=True) * (1.0 / TOKENS)

    def f_arrival(s):
        return remote(r.frecv.at[s], r.frecv.at[s], r.f_send.at[0, 0], r.f_recv.at[s], sib_dev)

    each(0, PL, lambda s: f_arrival(s).wait_recv())
    total = r.frecv[0].astype(F32)
    for s in range(1, PL):
        total = total + r.frecv[s].astype(F32)
    gl_out[...] = total[0:HS, :].T
    for w in range(HS // 128):
        gh_out[:, w * 128 : (w + 1) * 128] = total[HS + w * ES : HS + (w + 1) * ES, :]

    def f_sent(j):
        for c in (0, 1):

            @pl.when(jnp.logical_not(f_local(j, c)))
            def _():
                f_copy(j, c).wait_send()

    each(0, U, f_sent)


def solution(mesh):
    PL = mesh.shape["blk"]
    Z = mesh.shape["grp"] // 2
    M = 2 * Z
    K = len(PARTS)

    def on_device(series, positives, w_last, w_head, pair_index):
        TB, D = series.shape
        HS = w_last.shape[1]
        E = w_head.shape[1]
        DS, ES = D // PL, E // PL
        dims = (Z, PL, TB, D, HS, E, TB * PL * M)
        pair = pair_index.reshape(M, TB)
        vm, sem = pltpu.VMEM, pltpu.SemaphoreType.DMA
        rows = M * TB
        fr = HS + ES * (HS // 128)
        scratch = dict(
            xbuf=vm((rows, D), BF16),
            wbuf=vm((D, HS), BF16),
            whbuf=vm((HS, E), BF16),
            kbuf=vm((rows, E), BF16),
            prbuf=vm((PL // 2, M, TB), jnp.int32),
            hidt=vm((HS, rows), BF16),
            dgt=vm((HS, rows), F32),
            gbuf=vm((rows, E), BF16),
            dpt=vm((HS, rows), BF16),
            ghb=vm((E, HS), BF16),
            fsend=vm((PL // 2, 2, fr, DS), BF16),
            frecv=vm((PL, fr, DS), BF16),
            lplane=vm((PL, 8, 128), F32),
            lcol=vm((Z, 8, 128), F32),
            lsib=vm((2, 8, 128), F32),
            x_sem=sem((K,)),
            ls_send=sem,
            ls_recv=sem,
        )
        for k, n in enumerate(PARTS):
            for name in ("msend", "mrecv", "qbuf", "psend", "precv"):
                scratch[name + str(k)] = vm((PL, n, E), BF16)
            for name in ("tsend", "trecv"):
                scratch[name + str(k)] = vm((PL, 1, n * GROUPS[k]), F32)
            for name in ("hown", "hsend", "hsib"):
                scratch[name + str(k)] = vm((Z, n, E), F32)
            for name in ("hdir", "hrecv"):
                scratch[name + str(k)] = vm((Z, n, E), BF16)
            scratch["ubuf" + str(k)] = vm((n, E), F32)
            scratch["rnbuf" + str(k)] = vm((n, 128), F32)
        hops = Z // 2
        sems = dict(
            w=(2,), pr=(PL // 2,), m=(K, PL), hs=(K, Z), hd=(K, Z), q=(K, PL), p=(K, PL), t=(K, PL),
            gd=(K, Z), gs=(K, Z), lp=(PL,), lc=(Z,), f=(PL // 2, 2),
        )
        for name, chunks in [("k", KEY_CHUNKS)] + [("x%d" % k, c) for k, c in enumerate(CHUNKS)]:
            sems[name] = (2, hops * chunks)
            sems[name + "s"] = (2, hops * chunks + chunks // 2)
        for name, shape in sems.items():
            scratch[name + "_send"] = sem(shape)
            scratch[name + "_recv"] = sem((PL,) if name == "f" else shape)
        names = list(scratch)

        def body(*refs):
            kernel(dims, refs[:5], refs[5:8], types.SimpleNamespace(**dict(zip(names, refs[8:]))))

        any_spec = pl.BlockSpec(memory_space=pl.ANY)
        vm_spec = pl.BlockSpec(memory_space=pltpu.VMEM)
        loss, grad_last, grad_head = pl.pallas_call(
            body,
            out_shape=(
                jax.ShapeDtypeStruct((1, 1), F32),
                jax.ShapeDtypeStruct((DS, HS), F32),
                jax.ShapeDtypeStruct((ES, HS), F32),
            ),
            in_specs=[any_spec, vm_spec, any_spec, any_spec, vm_spec],
            out_specs=(vm_spec, vm_spec, vm_spec),
            scratch_shapes=list(scratch.values()),
            compiler_params=pltpu.CompilerParams(
                collective_id=0, has_side_effects=True, vmem_limit_bytes=VMEM_BYTES
            ),
        )(series, positives, w_last, w_head, pair)
        return (loss[0, 0], grad_last, grad_head.T)

    return jax.shard_map(
        on_device,
        mesh=mesh,
        in_specs=(
            P(("blk", "grp"), None),
            P(("blk", "grp"), None),
            P(None, "grp"),
            P("grp", None),
            P("blk"),
        ),
        out_specs=(P(), P("blk", "grp"), P("grp", "blk")),
        check_vma=False,
    )
```

```python
import functools
import math
import types

import jax
import jax.numpy as jnp
from jax import lax
from jax.experimental import pallas as pl
from jax.experimental.pallas import tpu as pltpu
from jax.sharding import PartitionSpec as P

MESH = pl.DeviceIdType.MESH
F32 = jnp.float32
BF16 = jnp.bfloat16

TEMP = 0.05
EPSILON = 1e-06
GELU_A = math.sqrt(2.0 / math.pi)
GELU_B = 0.044715
KEY_CHUNKS = 2
PARTS = (64, 64)
CHUNKS = (2, 2)
GROUPS = (4, 4)
VMEM_BYTES = 56 * 1024 * 1024


def dot_nn(left, right):
    return lax.dot_general(left, right, (((1,), (0,)), ((), ())), preferred_element_type=F32)


def dot_nt(left, right):
    return lax.dot_general(left, right, (((1,), (1,)), ((), ())), preferred_element_type=F32)


def fold_lanes(x):
    total = x[:, 0:128]
    for k in range(1, x.shape[1] // 128):
        total = total + x[:, k * 128 : (k + 1) * 128]
    return total


def kernel(dims, refs_in, refs_out, refs):
    Z, PL, TB, D, HS, E, TOKENS = dims
    series, positives, w_last, w_head, pair = refs_in
    (sums_out,) = refs_out
    r = refs
    U = PL // 2
    HOPS = Z // 2
    K = len(PARTS)
    first_row = [sum(PARTS[:k]) for k in range(K)]
    part_row = [2 * Z * f for f in first_row]
    group = GROUPS
    g_bits = [g.bit_length() - 1 for g in group]
    KEYS = 2 * Z * TB
    DS = D // PL
    ES = E // PL
    GRP_ROWS = 2 * Z * TB
    blk = lax.axis_index("blk")
    grp = lax.axis_index("grp")
    core = blk % 2
    xhi = grp % 2
    z = grp // 2
    uid = blk // 2
    pid = uid * 2 + xhi
    sib_blk = uid * 2 + 1 - core
    sib_dev = (sib_blk, grp)
    holder = core == xhi

    UB = U.bit_length() - 1
    ubits = [(uid // (1 << b)) % 2 for b in range(UB)]

    def flip(bit, by):
        if isinstance(by, int):
            return 1 - bit if by else bit
        return bit + by - 2 * bit * by

    def bits_of(j, count):
        if isinstance(j, int):
            return [(j >> b) & 1 for b in range(count)]
        out = []
        for b in reversed(range(count)):
            bit = jnp.where(j >= (1 << b), 1, 0)
            out.append(bit)
            j = j - bit * (1 << b)
        return out[::-1]

    def unit_z(i):
        t = z + ((i + 1) // 2) * (1 - 2 * (i % 2))
        return jnp.where(t < 0, t + Z, jnp.where(t >= Z, t - Z, t))

    def column(i):
        return (blk, unit_z(i) * 2 + xhi)

    def seen_from(i):
        return i if i in (0, Z - 1) else (i + 1 if i % 2 else i - 1)

    def unit_of(flips):
        return sum(flip(bit, by) * (1 << b) for b, (bit, by) in enumerate(zip(ubits, flips)))

    def unit_u(j):
        return unit_of(bits_of(j, UB))

    def plane(i, b=None, low=1):
        if b is None:
            b, i = i % 2, i // 2
        u = unit_of(bits_of(b // 2, low - 1) + bits_of(i, UB + 1 - low))
        return (u * 2 + core, z * 2 + flip(xhi, b % 2))

    def position(i):
        return i - 1 if 0 < i < Z - 1 else (Z - 2 if i == 0 else i)

    def remote(src, dst, ssem, rsem, dev):
        return pltpu.make_async_remote_copy(
            src_ref=src, dst_ref=dst, send_sem=ssem, recv_sem=rsem, device_id=dev, device_id_type=MESH
        )

    def each(low, high, body):
        def step(i, c):
            body(i)
            return c

        lax.fori_loop(low, high, step, 0)

    def parts_of(name):
        return [getattr(r, name + str(k)) for k in range(K)]

    msend, mrecv, qbuf, psend, precv, tsend, trecv = map(
        parts_of, ("msend", "mrecv", "qbuf", "psend", "precv", "tsend", "trecv")
    )
    hown, hsend, hsib, hdir, hrecv, ubuf, rnbuf = map(
        parts_of, ("hown", "hsend", "hsib", "hdir", "hrecv", "ubuf", "rnbuf")
    )

    barrier = pltpu.get_barrier_semaphore()

    def greet(dev):
        pl.semaphore_signal(barrier, inc=1, device_id=dev, device_id_type=MESH)

    greet(sib_dev)
    for i in range(1, Z):
        greet(column(i))
    for i in range(1, PL):
        greet(plane(i))
        greet((unit_u(i // 2) * 2 + xhi, z * 2 + flip(xhi, i % 2)))

    own_copies = [
        pltpu.make_async_copy(
            series.at[pl.ds(first_row[k], PARTS[k])],
            r.xbuf.at[pl.ds(part_row[k] + position(0) * 2 * PARTS[k], PARTS[k])],
            r.x_sem.at[k],
        )
        for k in range(K)
    ]
    for copy in own_copies:
        copy.start()
    key_float = positives[...].astype(F32)
    key_norm = jnp.sqrt(jnp.sum(key_float * key_float, axis=1, keepdims=True) + EPSILON)
    r.kbuf[position(0) * 2 * TB : position(0) * 2 * TB + TB, :] = (key_float / key_norm).astype(BF16)
    r.prbuf[0] = pair[...]

    pl.semaphore_wait(barrier, 1 + (Z - 1) + (PL - 1) + PL - 2 * jnp.where(holder, 1, 0))

    class Ring:
        def __init__(self, name, buf, base, rows, chunks, source):
            self.buf, self.base, self.rows, self.chunks, self.source = buf, base, rows, chunks, source
            self.sems = [getattr(r, name + s) for s in ("_send", "_recv", "s_send", "s_recv")]

        def place(self, direction, hop):
            return 0 if hop == 0 else min(2 * hop - 1 + direction, Z - 1)

        def chunk_list(self, direction, hop):
            half = self.chunks // 2
            if hop == HOPS:
                return list(range(half)) if direction == 0 else list(range(half, self.chunks))
            order = list(range(self.chunks))
            return order if direction == 0 else order[half:] + order[:half]

        def at(self, i, rel, chunk, count=1):
            size = self.rows // self.chunks
            return self.buf.at[pl.ds(self.base + (position(i) * 2 + rel) * self.rows + chunk * size, size * count)]

        def send(self, direction, hop, chunk):
            size = self.rows // self.chunks
            src = self.at(self.place(direction, hop), 0, chunk)
            if hop == 0 and self.source is not None:
                src = self.source.at[pl.ds(chunk * size, size)]
            k = hop * self.chunks + chunk
            return remote(
                src,
                self.at(self.place(direction, hop + 1), 0, chunk),
                self.sems[0].at[direction, k],
                self.sems[1].at[direction, k],
                column(1 + (1 - direction)),
            )

        def arrival(self, direction, hop, chunk):
            ref = self.at(self.place(direction, hop), 0, chunk)
            k = (hop - 1) * self.chunks + chunk
            return remote(ref, ref, self.sems[0].at[direction, k], self.sems[1].at[direction, k], sib_dev)

        def over(self, direction, hop, chunk, rel=0):
            i = self.place(direction, hop)
            k = (hop - 1) * self.chunks + chunk
            src = self.at(i, rel, chunk)
            return remote(
                src, self.at(i, 1, chunk), self.sems[2].at[direction, k], self.sems[3].at[direction, k], sib_dev
            )

        def over_own(self, rel=0):
            src = self.at(0, rel, 0, self.chunks)
            if rel == 0 and self.source is not None:
                src = self.source
            last = HOPS * self.chunks - self.chunks // 2 - 1 + self.chunks
            return remote(
                src, self.at(0, 1, 0, self.chunks), self.sems[2].at[0, last], self.sems[3].at[0, last], sib_dev
            )

        def begin_with(self, n):
            for direction in (0, 1):
                self.send(direction, 0, self.chunk_list(direction, 0)[n]).start()

        def begin(self):
            for n in range(self.chunks):
                self.begin_with(n)
            self.over_own().start()

        def passing(self, hop, n):
            for direction in (0, 1):
                chunk = self.chunk_list(direction, hop)[n]
                self.arrival(direction, hop, chunk).wait_recv()
                if hop + 1 <= HOPS and chunk in self.chunk_list(direction, hop + 1):
                    self.send(direction, hop, chunk).start()
                self.over(direction, hop, chunk).start()

        def passing_all(self, hop):
            for n in range(len(self.chunk_list(0, hop))):
                self.passing(hop, n)

        def other_ready(self, hop):
            for direction in (0, 1) if hop else ():
                for chunk in self.chunk_list(direction, hop):
                    self.over(direction, hop, chunk, 1).wait_recv()
            if hop == 0:
                self.over_own(1).wait_recv()

        def drain(self):
            for direction in (0, 1):
                for hop in range(HOPS + 1):
                    for chunk in self.chunk_list(direction, hop):
                        if hop < HOPS and chunk in self.chunk_list(direction, hop + 1):
                            self.send(direction, hop, chunk).wait_send()
                        if hop:
                            self.over(direction, hop, chunk).wait_send()
            self.over_own().wait_send()

    keys_ring = Ring("k", r.kbuf, 0, TB, KEY_CHUNKS, None)
    rings = [
        Ring("x%d" % k, r.xbuf, part_row[k], PARTS[k], CHUNKS[k], series.at[pl.ds(first_row[k], PARTS[k])])
        for k in range(K)
    ]
    keys_ring.begin()
    rings[0].begin_with(0)

    partner = (blk, z * 2 + 1 - xhi)
    w_copies = [
        remote(w_last, r.wbuf, r.w_send.at[0], r.w_recv.at[0], partner),
        remote(w_head, r.whbuf, r.w_send.at[1], r.w_recv.at[1], partner),
    ]

    @pl.when(holder)
    def _():
        for copy in w_copies:
            copy.start()
        pltpu.make_async_copy(w_last, r.wbuf, r.w_recv.at[0]).start()
        pltpu.make_async_copy(w_head, r.whbuf, r.w_recv.at[1]).start()

    def pair_copy(j):
        return remote(pair, r.prbuf.at[j], r.pr_send.at[j], r.pr_recv.at[j], plane(j * 2))

    for j in range(1, U):
        pair_copy(j).start()

    class Swap:
        def __init__(self, name, src, dst, k):
            self.src, self.dst, self.k = getattr(r, src + str(k)), getattr(r, dst + str(k)), k
            self.ssem, self.rsem = (getattr(r, name + s).at[k] for s in ("_send", "_recv"))

        def copy(self, i, b=None, own=False):
            k = i if b is None else i * group[self.k] + b
            dev = plane(i) if b is None else plane(i, b, g_bits[self.k])
            src = self.src.at[0 if own else k]
            return remote(src, self.dst.at[k], self.ssem.at[k], self.rsem.at[k], dev)

        def own_copy(self, i, b=None):
            return self.copy(i, b, True)

    swap_m = [Swap("m", "msend", "mrecv", k) for k in range(K)]
    swap_q = [Swap("q", "qbuf", "qbuf", k) for k in range(K)]
    swap_p = [Swap("p", "psend", "precv", k) for k in range(K)]
    swap_t = [Swap("t", "tsend", "trecv", k) for k in range(K)]

    def members(k, u, body):
        for b in range(group[k]):
            if b == 0:
                pl.when(u != 0)(functools.partial(body, u, b))
            else:
                body(u, b)

    def find_pairs(k, low, high):
        n, g = PARTS[k], group[k]
        UNIT = n * g

        def unit(u):
            lanes = lax.broadcasted_iota(jnp.int32, (UNIT, TB), 1)
            cols = []
            for b in range(g):
                row = r.prbuf[u * (g // 2) + b // 2, pl.ds(z * 2 + flip(xhi, b % 2), 1), :]
                cols.append(jnp.broadcast_to(row, (TB, TB)).T[first_row[k] : first_row[k] + n, :])
            both = jnp.concatenate(cols, axis=0) - lanes
            total = jnp.zeros((UNIT, E), F32)
            for i in range(Z):
                base = (unit_z(i) * 2 + xhi) * TB
                hot = jnp.concatenate([both == blk * GRP_ROWS + base, both == sib_blk * GRP_ROWS + base], axis=1)
                hot = jnp.where(hot, 1.0, 0.0).astype(BF16)
                at = position(i) * 2 * TB
                total = total + dot_nn(hot, r.kbuf[at : at + 2 * TB, :])
            for b in range(g):
                msend[k][u * g + b] = total[b * n : (b + 1) * n, :].astype(BF16)
            members(k, u, lambda *at: swap_m[k].copy(*at).start())

        each(low, high, unit)

    def places(hops):
        out = []
        for hop in hops:
            out += [0] if hop == 0 else ([Z - 1] if hop == HOPS else [2 * hop - 1, 2 * hop])
        return out

    def span(k, hops):
        at = [position(i) for i in places(hops)]
        return part_row[k] + at[0] * 2 * PARTS[k], part_row[k] + (at[-1] + 1) * 2 * PARTS[k]

    def hs_copy(k, i):
        return remote(hsend[k].at[i], hsib[k].at[i], r.hs_send.at[k, i], r.hs_recv.at[k, i], sib_dev)

    def hd_copy(k, i):
        slot = seen_from(i)
        return remote(hdir[k].at[i], hrecv[k].at[slot], r.hd_send.at[k, i], r.hd_recv.at[k, slot], column(i))

    def encode(k, *hops):
        n = PARTS[k]
        for hop in hops:
            rings[k].other_ready(hop)
        start, stop = span(k, hops)
        x = dot_nn(r.xbuf[start:stop, :], r.wbuf[...])
        x2 = x * x
        t = jnp.tanh(GELU_A * (x + GELU_B * (x2 * x)))
        cdf = 0.5 + 0.5 * t
        hidden = x * cdf
        out = dot_nn(hidden.astype(BF16), r.whbuf[...])
        for m, i in enumerate(places(hops)):
            hown[k][i] = out[m * 2 * n : m * 2 * n + n, :]
            hsend[k][i] = out[m * 2 * n + n : (m + 1) * 2 * n, :]
            hs_copy(k, i).start()
        r.hidt[:, start:stop] = hidden.T.astype(BF16)
        dgelu = cdf + (0.5 * GELU_A) * x * (1.0 - t * t) * (1.0 + (3.0 * GELU_B) * x2)
        r.dgt[:, start:stop] = dgelu.T

    def head_send(k, *hops):
        for i in places(hops):
            if i:
                hs_copy(k, i).wait_recv()
                hdir[k][i] = (hown[k][i] + hsib[k][i]).astype(BF16)
                hd_copy(k, i).start()

    def make_queries(k):
        hs_copy(k, 0).wait_recv()
        head = hown[k][0] + hsib[k][0]
        for i in range(1, Z):
            hd_copy(k, seen_from(i)).wait_recv()
            head = head + hrecv[k][i].astype(F32)
        row_norm = jnp.sqrt(jnp.sum(head * head, axis=1, keepdims=True) + EPSILON)
        unit_rows = head / row_norm
        ubuf[k][...] = unit_rows
        rnbuf[k][...] = jnp.broadcast_to(row_norm, (PARTS[k], 128))
        qbuf[k][0] = unit_rows.astype(BF16)
        for i in range(1, PL):
            swap_q[k].own_copy(i).start()

    CHUNK = min(512, KEYS)
    scale = (1.0 / TEMP) * math.log2(math.e)

    def attend(k, low, high):
        n, g = PARTS[k], group[k]
        UNIT = n * g

        def unit(u):
            members(k, u, lambda *at: swap_q[k].own_copy(*at).wait_recv())
            q = qbuf[k][pl.ds(u * g, g)].reshape(UNIT, E)
            total = jnp.zeros((UNIT, 128), F32)
            weighted = jnp.zeros((UNIT, E), F32)
            for c in range(KEYS // CHUNK):
                keys = r.kbuf[c * CHUNK : (c + 1) * CHUNK, :]
                e = jnp.exp2(dot_nt(q, keys) * scale)
                total = total + fold_lanes(e)
                weighted = weighted + dot_nn(e.astype(BF16), keys)
            for b in range(g):
                psend[k][u * g + b] = weighted[b * n : (b + 1) * n, :].astype(BF16)
            members(k, u, lambda *at: swap_p[k].copy(*at).start())
            part = jnp.sum(total.T, axis=0, keepdims=True)
            for b in range(g):
                tsend[k][u * g + b] = part
            members(k, u, lambda *at: swap_t[k].copy(*at).start())

        each(low, high, unit)

    def g_rows(k, i, rel):
        return r.gbuf.at[pl.ds(part_row[k] + (position(i) * 2 + rel) * PARTS[k], PARTS[k])]

    def g_direct(k, i):
        slot = seen_from(i)
        return remote(g_rows(k, 0, 0), g_rows(k, slot, 0), r.gd_send.at[k, i], r.gd_recv.at[k, slot], column(i))

    def g_arrival(k, i):
        ref = g_rows(k, i, 0)
        return remote(ref, ref, r.gd_send.at[k, i], r.gd_recv.at[k, i], sib_dev)

    def g_over(k, i, rel=0):
        return remote(g_rows(k, i, rel), g_rows(k, i, 1), r.gs_send.at[k, i], r.gs_recv.at[k, i], sib_dev)

    def make_rows(k):
        n, g = PARTS[k], group[k]
        UNIT = n * g
        matched = msend[k][0].astype(F32)
        for i in range(1, PL):
            swap_m[k].copy(i).wait_recv()
            matched = matched + mrecv[k][i].astype(F32)
        weighted = psend[k][0].astype(F32)
        lanes = lax.broadcasted_iota(jnp.int32, (1, UNIT), 1)
        side = [jnp.logical_and(lanes >= b * n, lanes < (b + 1) * n) for b in range(g)]
        totals = jnp.where(side[0], tsend[k][0], 0.0)
        for i in range(1, PL):
            swap_p[k].copy(i).wait_recv()
            swap_t[k].copy(i).wait_recv()
            weighted = weighted + precv[k][i].astype(F32)
            totals = totals + jnp.where(side[i % g], trecv[k][i], 0.0)
        column_totals = jnp.broadcast_to(totals, (128, UNIT)).T
        total = column_totals[0:n, :]
        for b in range(1, g):
            total = total + column_totals[b * n : (b + 1) * n, :]
        wide = jnp.concatenate([total] * (E // 128), axis=1)
        grad = (weighted / wide - matched) * (1.0 / TEMP)
        unit_rows = ubuf[k][...]
        along = jnp.sum(unit_rows * grad, axis=1, keepdims=True)
        norm = jnp.concatenate([rnbuf[k][...]] * (E // 128), axis=1)
        g_rows(k, 0, 0)[...] = ((grad - unit_rows * along) / norm).astype(BF16)
        g_over(k, 0).start()
        for i in range(1, Z):
            g_direct(k, i).start()
        hit = qbuf[k][0].astype(F32) * matched
        hit = fold_lanes(jnp.sum(hit.reshape(n // 8, 8, E), axis=0))
        logs = jnp.sum(jnp.log(total).reshape(n // 8, 8, 128), axis=0)
        first = lax.broadcasted_iota(jnp.int32, (8, 128), 1) == 0
        return jnp.where(first, logs, 0.0) - hit * (1.0 / TEMP)

    def back(k, *hops):
        for i in places(hops):
            if i:
                g_arrival(k, i).wait_recv()
                g_over(k, i).start()
        for i in places(hops):
            g_over(k, i, 1).wait_recv()
        start, stop = span(k, hops)
        dp = dot_nt(r.whbuf[...], r.gbuf[start:stop, :]) * r.dgt[:, start:stop]
        r.dpt[:, start:stop] = dp.astype(BF16)

    def lp_copy(i):
        return remote(r.lplane.at[pid], r.lplane.at[pid], r.lp_send.at[i], r.lp_recv.at[i], plane(i))

    def lp_arrival(i):
        p = unit_u(i // 2) * 2 + flip(xhi, i % 2)
        return remote(r.lplane.at[p], r.lplane.at[p], r.lp_send.at[i], r.lp_recv.at[i], sib_dev)

    def lc_copy(i):
        ref = r.lcol.at[z]
        return remote(ref, ref, r.lc_send.at[i], r.lc_recv.at[seen_from(i)], column(i))

    def lc_arrival(i):
        ref = r.lcol.at[unit_z(i)]
        return remote(ref, ref, r.lc_send.at[i], r.lc_recv.at[i], sib_dev)

    def ls_copy(c):
        return remote(r.lsib.at[c], r.lsib.at[c], r.ls_send, r.ls_recv, sib_dev)

    for copy in own_copies:
        copy.wait()
    keys_ring.passing_all(1)
    rings[0].begin_with(1)
    rings[0].over_own().start()
    keys_ring.passing_all(2)
    rings[0].passing(1, 0)
    keys_ring.passing_all(3)
    rings[0].passing(1, 1)
    keys_ring.passing_all(4)
    rings[0].passing(2, 0)
    for j in range(1, U):
        pair_copy(j).wait_recv()
    for hop in range(HOPS + 1):
        keys_ring.other_ready(hop)
    find_pairs(0, 0, 2)
    rings[0].passing(2, 1)
    find_pairs(0, 2, 4)
    rings[0].passing(3, 0)
    find_pairs(1, 0, 2)
    rings[0].passing(3, 1)
    rings[1].begin()
    find_pairs(1, 2, 4)
    for copy in w_copies:
        copy.wait_recv()
    encode(0, 1)
    encode(0, 2)
    rings[0].passing_all(4)
    encode(0, 3)
    head_send(0, 1, 2)
    encode(0, 0, 4)
    head_send(0, 3, 0, 4)
    rings[1].passing_all(1)
    rings[1].passing_all(2)
    encode(1, 1)
    rings[1].passing_all(3)
    encode(1, 2)
    make_queries(0)
    rings[1].passing_all(4)
    encode(1, 3)
    encode(1, 0, 4)
    head_send(1, 1, 2, 3, 0, 4)
    attend(0, 0, 4)
    make_queries(1)
    loss = make_rows(0)
    attend(1, 0, 4)
    back(0, 1, 2)
    back(0, 3, 0, 4)
    loss = loss + make_rows(1)
    r.lplane[pid] = loss
    for i in range(1, PL):
        lp_copy(i).start()
    back(1, 1, 2)
    back(1, 3, 0, 4)

    ghead = dot_nn(r.hidt[...], r.gbuf[...])
    r.ghb[...] = ghead.T.astype(BF16)

    for i in range(1, PL):
        lp_arrival(i).wait_recv()
    loss = r.lplane[0]
    for p in range(1, PL):
        loss = loss + r.lplane[p]
    r.lcol[z] = loss
    for i in range(1, Z):
        lc_copy(i).start()

    def f_copy(j, c):
        slot = j * 2 + jnp.where(holder, 0, 1)
        return remote(
            r.fsend.at[j, c],
            r.frecv.at[slot],
            r.f_send.at[j, c],
            r.f_recv.at[slot],
            (unit_u(j) * 2 + c, z * 2 + core),
        )

    def f_local(j, c):
        return jnp.logical_and(jnp.logical_and(holder, j == 0), c == core)

    def last(step):
        j = U - 1 - step
        n = unit_u(j)
        cols = pl.ds(pl.multiple_of(n * 2 * DS, 2 * DS), 2 * DS)
        part = dot_nn(r.dpt[...], r.xbuf[:, cols]).astype(BF16)
        for c in (0, 1):
            d = n * 2 + c
            r.fsend[j, c, 0:HS, :] = part[:, c * DS : (c + 1) * DS]
            gh = r.ghb[pl.ds(pl.multiple_of(d * ES, 16), ES), :]
            for w in range(HS // 128):
                r.fsend[j, c, HS + w * ES : HS + (w + 1) * ES, :] = gh[:, w * 128 : (w + 1) * 128]

            @pl.when(jnp.logical_not(f_local(j, c)))
            def _():
                f_copy(j, c).start()

            @pl.when(f_local(j, c))
            def _():
                pltpu.make_async_copy(r.fsend.at[j, c], r.frecv.at[0], r.f_recv.at[0]).start()

    each(0, U, last)

    for i in range(1, Z):
        lc_arrival(i).wait_recv()
    loss = r.lcol[0]
    for p in range(1, Z):
        loss = loss + r.lcol[p]
    r.lsib[core] = loss
    ls_copy(core).start()

    for ring in [keys_ring] + rings:
        ring.drain()

    @pl.when(holder)
    def _():
        for copy in w_copies:
            copy.wait_send()

    for j in range(1, U):
        pair_copy(j).wait_send()
    for k in range(K):
        for i in range(Z):
            hs_copy(k, i).wait_send()
            g_over(k, i).wait_send()
            if i:
                hd_copy(k, i).wait_send()
                g_direct(k, i).wait_send()
        for i in range(1, PL):
            swap_q[k].own_copy(i).wait_send()
            swap_m[k].copy(i).wait_send()
            swap_p[k].copy(i).wait_send()
            swap_t[k].copy(i).wait_send()
    for i in range(1, PL):
        lp_copy(i).wait_send()
    for i in range(1, Z):
        lc_copy(i).wait_send()

    ls_copy(1 - core).wait_recv()
    ls_copy(core).wait_send()
    loss = r.lsib[0] + r.lsib[1]
    loss = jnp.sum(loss, axis=1, keepdims=True)
    loss = jnp.sum(loss, axis=0, keepdims=True) * (1.0 / TOKENS)
    sums = HS + ES * (HS // 128)
    sums_out[sums : sums + 8, :] = jnp.broadcast_to(loss, (8, DS))

    def f_arrival(s):
        return remote(r.frecv.at[s], r.frecv.at[s], r.f_send.at[0, 0], r.f_recv.at[s], sib_dev)

    each(0, PL, lambda s: f_arrival(s).wait_recv())
    total = r.frecv[0].astype(F32)
    for s in range(1, PL):
        total = total + r.frecv[s].astype(F32)
    sums_out[0:sums, :] = total

    def f_sent(j):
        for c in (0, 1):

            @pl.when(jnp.logical_not(f_local(j, c)))
            def _():
                f_copy(j, c).wait_send()

    each(0, U, f_sent)


def finish(sums, loss_out, gl_out, gh_out):
    HS, (ES, _) = gl_out.shape[1], gh_out.shape
    gl_out[...] = sums[0:HS, :].T
    for w in range(HS // 128):
        gh_out[:, w * 128 : (w + 1) * 128] = sums[HS + w * ES : HS + (w + 1) * ES, :]
    end = HS + ES * (HS // 128)
    loss_out[...] = sums[end : end + 1, 0:1]


def solution(mesh):
    PL = mesh.shape["blk"]
    Z = mesh.shape["grp"] // 2
    M = 2 * Z
    K = len(PARTS)

    def on_device(series, positives, w_last, w_head, pair_index):
        TB, D = series.shape
        HS = w_last.shape[1]
        E = w_head.shape[1]
        DS, ES = D // PL, E // PL
        dims = (Z, PL, TB, D, HS, E, TB * PL * M)
        pair = pair_index.reshape(M, TB)
        vm, sem = pltpu.VMEM, pltpu.SemaphoreType.DMA
        rows = M * TB
        fr = HS + ES * (HS // 128)
        scratch = dict(
            xbuf=vm((rows, D), BF16),
            wbuf=vm((D, HS), BF16),
            whbuf=vm((HS, E), BF16),
            kbuf=vm((rows, E), BF16),
            prbuf=vm((PL // 2, M, TB), jnp.int32),
            hidt=vm((HS, rows), BF16),
            dgt=vm((HS, rows), F32),
            gbuf=vm((rows, E), BF16),
            dpt=vm((HS, rows), BF16),
            ghb=vm((E, HS), BF16),
            fsend=vm((PL // 2, 2, fr, DS), BF16),
            frecv=vm((PL, fr, DS), BF16),
            lplane=vm((PL, 8, 128), F32),
            lcol=vm((Z, 8, 128), F32),
            lsib=vm((2, 8, 128), F32),
            x_sem=sem((K,)),
            ls_send=sem,
            ls_recv=sem,
        )
        for k, n in enumerate(PARTS):
            for name in ("msend", "mrecv", "qbuf", "psend", "precv"):
                scratch[name + str(k)] = vm((PL, n, E), BF16)
            for name in ("tsend", "trecv"):
                scratch[name + str(k)] = vm((PL, 1, n * GROUPS[k]), F32)
            for name in ("hown", "hsend", "hsib"):
                scratch[name + str(k)] = vm((Z, n, E), F32)
            for name in ("hdir", "hrecv"):
                scratch[name + str(k)] = vm((Z, n, E), BF16)
            scratch["ubuf" + str(k)] = vm((n, E), F32)
            scratch["rnbuf" + str(k)] = vm((n, 128), F32)
        hops = Z // 2
        sems = dict(
            w=(2,), pr=(PL // 2,), m=(K, PL), hs=(K, Z), hd=(K, Z), q=(K, PL), p=(K, PL), t=(K, PL),
            gd=(K, Z), gs=(K, Z), lp=(PL,), lc=(Z,), f=(PL // 2, 2),
        )
        for name, chunks in [("k", KEY_CHUNKS)] + [("x%d" % k, c) for k, c in enumerate(CHUNKS)]:
            sems[name] = (2, hops * chunks)
            sems[name + "s"] = (2, hops * chunks + chunks // 2)
        for name, shape in sems.items():
            scratch[name + "_send"] = sem(shape)
            scratch[name + "_recv"] = sem((PL,) if name == "f" else shape)
        names = list(scratch)

        def body(*refs):
            kernel(dims, refs[:5], refs[5:6], types.SimpleNamespace(**dict(zip(names, refs[6:]))))

        any_spec = pl.BlockSpec(memory_space=pl.ANY)
        vm_spec = pl.BlockSpec(memory_space=pltpu.VMEM)
        (sums,) = pl.pallas_call(
            body,
            out_shape=(pltpu.VMEM((fr + 8, DS), F32),),
            in_specs=[any_spec, vm_spec, any_spec, any_spec, vm_spec],
            out_specs=(vm_spec,),
            scratch_shapes=list(scratch.values()),
            compiler_params=pltpu.CompilerParams(
                collective_id=0, has_side_effects=True, vmem_limit_bytes=VMEM_BYTES
            ),
        )(series, positives, w_last, w_head, pair)
        loss, grad_last, grad_head = pl.pallas_call(
            finish,
            out_shape=(
                jax.ShapeDtypeStruct((1, 1), F32),
                jax.ShapeDtypeStruct((DS, HS), F32),
                jax.ShapeDtypeStruct((ES, HS), F32),
            ),
            in_specs=[vm_spec],
            out_specs=(vm_spec, vm_spec, vm_spec),
        )(sums)
        return (loss[0, 0], grad_last, grad_head.T)

    return jax.shard_map(
        on_device,
        mesh=mesh,
        in_specs=(
            P(("blk", "grp"), None),
            P(("blk", "grp"), None),
            P(None, "grp"),
            P("grp", None),
            P("blk"),
        ),
        out_specs=(P(), P("blk", "grp"), P("grp", "blk")),
        check_vma=False,
    )
```

```python
import functools
import math
import types

import jax
import jax.numpy as jnp
from jax import lax
from jax.experimental import pallas as pl
from jax.experimental.pallas import tpu as pltpu
from jax.sharding import PartitionSpec as P

MESH = pl.DeviceIdType.MESH
F32 = jnp.float32
BF16 = jnp.bfloat16

TEMP = 0.05
EPSILON = 1e-06
GELU_A = math.sqrt(2.0 / math.pi)
GELU_B = 0.044715
KEY_CHUNKS = 2
PARTS = (64, 64)
CHUNKS = (2, 2)
GROUPS = (4, 4)
VMEM_BYTES = 56 * 1024 * 1024


def dot_nn(left, right):
    return lax.dot_general(left, right, (((1,), (0,)), ((), ())), preferred_element_type=F32)


def dot_nt(left, right):
    return lax.dot_general(left, right, (((1,), (1,)), ((), ())), preferred_element_type=F32)


def fold_lanes(x):
    total = x[:, 0:128]
    for k in range(1, x.shape[1] // 128):
        total = total + x[:, k * 128 : (k + 1) * 128]
    return total


def kernel(dims, refs_in, refs_out, refs):
    Z, PL, TB, D, HS, E, TOKENS = dims
    series, positives, w_last, w_head, pair = refs_in
    (sums_out,) = refs_out
    r = refs
    U = PL // 2
    HOPS = Z // 2
    K = len(PARTS)
    first_row = [sum(PARTS[:k]) for k in range(K)]
    part_row = [2 * Z * f for f in first_row]
    group = GROUPS
    g_bits = [g.bit_length() - 1 for g in group]
    KEYS = 2 * Z * TB
    DS = D // PL
    ES = E // PL
    GRP_ROWS = 2 * Z * TB
    blk = lax.axis_index("blk")
    grp = lax.axis_index("grp")
    core = blk % 2
    xhi = grp % 2
    z = grp // 2
    uid = blk // 2
    pid = uid * 2 + xhi
    sib_blk = uid * 2 + 1 - core
    sib_dev = (sib_blk, grp)
    holder = core == xhi

    UB = U.bit_length() - 1
    ubits = [(uid // (1 << b)) % 2 for b in range(UB)]

    def flip(bit, by):
        if isinstance(by, int):
            return 1 - bit if by else bit
        return bit + by - 2 * bit * by

    def bits_of(j, count):
        if isinstance(j, int):
            return [(j >> b) & 1 for b in range(count)]
        out = []
        for b in reversed(range(count)):
            bit = jnp.where(j >= (1 << b), 1, 0)
            out.append(bit)
            j = j - bit * (1 << b)
        return out[::-1]

    def unit_z(i):
        t = z + ((i + 1) // 2) * (1 - 2 * (i % 2))
        return jnp.where(t < 0, t + Z, jnp.where(t >= Z, t - Z, t))

    def column(i):
        return (blk, unit_z(i) * 2 + xhi)

    def seen_from(i):
        return i if i in (0, Z - 1) else (i + 1 if i % 2 else i - 1)

    def unit_of(flips):
        return sum(flip(bit, by) * (1 << b) for b, (bit, by) in enumerate(zip(ubits, flips)))

    def unit_u(j):
        return unit_of(bits_of(j, UB))

    def plane(i, b=None, low=1):
        if b is None:
            b, i = i % 2, i // 2
        u = unit_of(bits_of(b // 2, low - 1) + bits_of(i, UB + 1 - low))
        return (u * 2 + core, z * 2 + flip(xhi, b % 2))

    def position(i):
        return i - 1 if 0 < i < Z - 1 else (Z - 2 if i == 0 else i)

    def remote(src, dst, ssem, rsem, dev):
        return pltpu.make_async_remote_copy(
            src_ref=src, dst_ref=dst, send_sem=ssem, recv_sem=rsem, device_id=dev, device_id_type=MESH
        )

    def each(low, high, body):
        def step(i, c):
            body(i)
            return c

        lax.fori_loop(low, high, step, 0)

    def parts_of(name):
        return [getattr(r, name + str(k)) for k in range(K)]

    msend, mrecv, qbuf, psend, precv, tsend, trecv = map(
        parts_of, ("msend", "mrecv", "qbuf", "psend", "precv", "tsend", "trecv")
    )
    hown, hsend, hsib, hdir, hrecv, ubuf, rnbuf = map(
        parts_of, ("hown", "hsend", "hsib", "hdir", "hrecv", "ubuf", "rnbuf")
    )

    barrier = pltpu.get_barrier_semaphore()

    def greet(dev):
        pl.semaphore_signal(barrier, inc=1, device_id=dev, device_id_type=MESH)

    greet(sib_dev)
    for i in range(1, Z):
        greet(column(i))
    for i in range(1, PL):
        greet(plane(i))
        greet((unit_u(i // 2) * 2 + xhi, z * 2 + flip(xhi, i % 2)))

    own_copies = [
        pltpu.make_async_copy(
            series.at[pl.ds(first_row[k], PARTS[k])],
            r.xbuf.at[pl.ds(part_row[k] + position(0) * 2 * PARTS[k], PARTS[k])],
            r.x_sem.at[k],
        )
        for k in range(K)
    ]
    for copy in own_copies:
        copy.start()
    key_float = positives[...].astype(F32)
    key_norm = jnp.sqrt(jnp.sum(key_float * key_float, axis=1, keepdims=True) + EPSILON)
    r.kbuf[position(0) * 2 * TB : position(0) * 2 * TB + TB, :] = (key_float / key_norm).astype(BF16)
    r.prbuf[0] = pair[...]

    pl.semaphore_wait(barrier, 1 + (Z - 1) + (PL - 1) + PL - 2 * jnp.where(holder, 1, 0))

    class Ring:
        def __init__(self, name, buf, base, rows, chunks, source):
            self.buf, self.base, self.rows, self.chunks, self.source = buf, base, rows, chunks, source
            self.sems = [getattr(r, name + s) for s in ("_send", "_recv", "s_send", "s_recv")]

        def place(self, direction, hop):
            return 0 if hop == 0 else min(2 * hop - 1 + direction, Z - 1)

        def chunk_list(self, direction, hop):
            half = self.chunks // 2
            if hop == HOPS:
                return list(range(half)) if direction == 0 else list(range(half, self.chunks))
            order = list(range(self.chunks))
            return order if direction == 0 else order[half:] + order[:half]

        def at(self, i, rel, chunk, count=1):
            size = self.rows // self.chunks
            return self.buf.at[pl.ds(self.base + (position(i) * 2 + rel) * self.rows + chunk * size, size * count)]

        def send(self, direction, hop, chunk):
            size = self.rows // self.chunks
            src = self.at(self.place(direction, hop), 0, chunk)
            if hop == 0 and self.source is not None:
                src = self.source.at[pl.ds(chunk * size, size)]
            k = hop * self.chunks + chunk
            return remote(
                src,
                self.at(self.place(direction, hop + 1), 0, chunk),
                self.sems[0].at[direction, k],
                self.sems[1].at[direction, k],
                column(1 + (1 - direction)),
            )

        def arrival(self, direction, hop, chunk):
            ref = self.at(self.place(direction, hop), 0, chunk)
            k = (hop - 1) * self.chunks + chunk
            return remote(ref, ref, self.sems[0].at[direction, k], self.sems[1].at[direction, k], sib_dev)

        def over(self, direction, hop, chunk, rel=0):
            i = self.place(direction, hop)
            k = (hop - 1) * self.chunks + chunk
            src = self.at(i, rel, chunk)
            return remote(
                src, self.at(i, 1, chunk), self.sems[2].at[direction, k], self.sems[3].at[direction, k], sib_dev
            )

        def over_own(self, rel=0):
            src = self.at(0, rel, 0, self.chunks)
            if rel == 0 and self.source is not None:
                src = self.source
            last = HOPS * self.chunks - self.chunks // 2 - 1 + self.chunks
            return remote(
                src, self.at(0, 1, 0, self.chunks), self.sems[2].at[0, last], self.sems[3].at[0, last], sib_dev
            )

        def begin_with(self, n):
            for direction in (0, 1):
                self.send(direction, 0, self.chunk_list(direction, 0)[n]).start()

        def begin(self):
            for n in range(self.chunks):
                self.begin_with(n)
            self.over_own().start()

        def passing(self, hop, n):
            for direction in (0, 1):
                chunk = self.chunk_list(direction, hop)[n]
                self.arrival(direction, hop, chunk).wait_recv()
                if hop + 1 <= HOPS and chunk in self.chunk_list(direction, hop + 1):
                    self.send(direction, hop, chunk).start()
                self.over(direction, hop, chunk).start()

        def passing_all(self, hop):
            for n in range(len(self.chunk_list(0, hop))):
                self.passing(hop, n)

        def other_ready(self, hop):
            for direction in (0, 1) if hop else ():
                for chunk in self.chunk_list(direction, hop):
                    self.over(direction, hop, chunk, 1).wait_recv()
            if hop == 0:
                self.over_own(1).wait_recv()

        def drain(self):
            for direction in (0, 1):
                for hop in range(HOPS + 1):
                    for chunk in self.chunk_list(direction, hop):
                        if hop < HOPS and chunk in self.chunk_list(direction, hop + 1):
                            self.send(direction, hop, chunk).wait_send()
                        if hop:
                            self.over(direction, hop, chunk).wait_send()
            self.over_own().wait_send()

    keys_ring = Ring("k", r.kbuf, 0, TB, KEY_CHUNKS, None)
    rings = [
        Ring("x%d" % k, r.xbuf, part_row[k], PARTS[k], CHUNKS[k], series.at[pl.ds(first_row[k], PARTS[k])])
        for k in range(K)
    ]
    keys_ring.begin()
    rings[0].begin_with(0)

    partner = (blk, z * 2 + 1 - xhi)
    w_copies = [
        remote(w_last, r.wbuf, r.w_send.at[0], r.w_recv.at[0], partner),
        remote(w_head, r.whbuf, r.w_send.at[1], r.w_recv.at[1], partner),
    ]

    @pl.when(holder)
    def _():
        for copy in w_copies:
            copy.start()
        pltpu.make_async_copy(w_last, r.wbuf, r.w_recv.at[0]).start()
        pltpu.make_async_copy(w_head, r.whbuf, r.w_recv.at[1]).start()

    def pair_copy(j):
        return remote(pair, r.prbuf.at[j], r.pr_send.at[j], r.pr_recv.at[j], plane(j * 2))

    for j in range(1, U):
        pair_copy(j).start()

    class Swap:
        def __init__(self, name, src, dst, k):
            self.src, self.dst, self.k = getattr(r, src + str(k)), getattr(r, dst + str(k)), k
            self.ssem, self.rsem = (getattr(r, name + s).at[k] for s in ("_send", "_recv"))

        def copy(self, i, b=None, own=False):
            k = i if b is None else i * group[self.k] + b
            dev = plane(i) if b is None else plane(i, b, g_bits[self.k])
            src = self.src.at[0 if own else k]
            return remote(src, self.dst.at[k], self.ssem.at[k], self.rsem.at[k], dev)

        def own_copy(self, i, b=None):
            return self.copy(i, b, True)

    swap_m = [Swap("m", "msend", "mrecv", k) for k in range(K)]
    swap_q = [Swap("q", "qbuf", "qbuf", k) for k in range(K)]
    swap_p = [Swap("p", "psend", "precv", k) for k in range(K)]
    swap_t = [Swap("t", "tsend", "trecv", k) for k in range(K)]

    def members(k, u, body):
        for b in range(group[k]):
            if b == 0:
                pl.when(u != 0)(functools.partial(body, u, b))
            else:
                body(u, b)

    def find_pairs(k, low, high):
        n, g = PARTS[k], group[k]
        UNIT = n * g

        def unit(u):
            lanes = lax.broadcasted_iota(jnp.int32, (UNIT, TB), 1)
            cols = []
            for b in range(g):
                row = r.prbuf[u * (g // 2) + b // 2, pl.ds(z * 2 + flip(xhi, b % 2), 1), :]
                cols.append(jnp.broadcast_to(row, (TB, TB)).T[first_row[k] : first_row[k] + n, :])
            both = jnp.concatenate(cols, axis=0) - lanes
            total = jnp.zeros((UNIT, E), F32)
            for i in range(Z):
                base = (unit_z(i) * 2 + xhi) * TB
                hot = jnp.concatenate([both == blk * GRP_ROWS + base, both == sib_blk * GRP_ROWS + base], axis=1)
                hot = jnp.where(hot, 1.0, 0.0).astype(BF16)
                at = position(i) * 2 * TB
                total = total + dot_nn(hot, r.kbuf[at : at + 2 * TB, :])
            for b in range(g):
                msend[k][u * g + b] = total[b * n : (b + 1) * n, :].astype(BF16)
            members(k, u, lambda *at: swap_m[k].copy(*at).start())

        each(low, high, unit)

    def places(hops):
        out = []
        for hop in hops:
            out += [0] if hop == 0 else ([Z - 1] if hop == HOPS else [2 * hop - 1, 2 * hop])
        return out

    def span(k, hops):
        at = [position(i) for i in places(hops)]
        return part_row[k] + at[0] * 2 * PARTS[k], part_row[k] + (at[-1] + 1) * 2 * PARTS[k]

    def hs_copy(k, i):
        return remote(hsend[k].at[i], hsib[k].at[i], r.hs_send.at[k, i], r.hs_recv.at[k, i], sib_dev)

    def hd_copy(k, i):
        slot = seen_from(i)
        return remote(hdir[k].at[i], hrecv[k].at[slot], r.hd_send.at[k, i], r.hd_recv.at[k, slot], column(i))

    def encode(k, *hops):
        n = PARTS[k]
        for hop in hops:
            rings[k].other_ready(hop)
        start, stop = span(k, hops)
        x = dot_nn(r.xbuf[start:stop, :], r.wbuf[...])
        x2 = x * x
        t = jnp.tanh(GELU_A * (x + GELU_B * (x2 * x)))
        cdf = 0.5 + 0.5 * t
        hidden = x * cdf
        out = dot_nn(hidden.astype(BF16), r.whbuf[...])
        for m, i in enumerate(places(hops)):
            hown[k][i] = out[m * 2 * n : m * 2 * n + n, :]
            hsend[k][i] = out[m * 2 * n + n : (m + 1) * 2 * n, :]
            hs_copy(k, i).start()
        r.hidt[:, start:stop] = hidden.T.astype(BF16)
        dgelu = cdf + (0.5 * GELU_A) * x * (1.0 - t * t) * (1.0 + (3.0 * GELU_B) * x2)
        r.dgt[:, start:stop] = dgelu.T

    def head_send(k, *hops):
        for i in places(hops):
            if i:
                hs_copy(k, i).wait_recv()
                hdir[k][i] = (hown[k][i] + hsib[k][i]).astype(BF16)
                hd_copy(k, i).start()

    def make_queries(k):
        hs_copy(k, 0).wait_recv()
        head = hown[k][0] + hsib[k][0]
        for i in range(1, Z):
            hd_copy(k, seen_from(i)).wait_recv()
            head = head + hrecv[k][i].astype(F32)
        row_norm = jnp.sqrt(jnp.sum(head * head, axis=1, keepdims=True) + EPSILON)
        unit_rows = head / row_norm
        ubuf[k][...] = unit_rows
        rnbuf[k][...] = jnp.broadcast_to(row_norm, (PARTS[k], 128))
        qbuf[k][0] = unit_rows.astype(BF16)
        for i in range(1, PL):
            swap_q[k].own_copy(i).start()

    CHUNK = min(512, KEYS)
    scale = (1.0 / TEMP) * math.log2(math.e)

    def attend(k, low, high):
        n, g = PARTS[k], group[k]
        UNIT = n * g

        def unit(u):
            members(k, u, lambda *at: swap_q[k].own_copy(*at).wait_recv())
            q = qbuf[k][pl.ds(u * g, g)].reshape(UNIT, E)
            total = jnp.zeros((UNIT, 128), F32)
            weighted = jnp.zeros((UNIT, E), F32)
            for c in range(KEYS // CHUNK):
                keys = r.kbuf[c * CHUNK : (c + 1) * CHUNK, :]
                e = jnp.exp2(dot_nt(q, keys) * scale)
                total = total + fold_lanes(e)
                weighted = weighted + dot_nn(e.astype(BF16), keys)
            for b in range(g):
                psend[k][u * g + b] = weighted[b * n : (b + 1) * n, :].astype(BF16)
            members(k, u, lambda *at: swap_p[k].copy(*at).start())
            part = jnp.sum(total.T, axis=0, keepdims=True)
            for b in range(g):
                tsend[k][u * g + b] = part
            members(k, u, lambda *at: swap_t[k].copy(*at).start())

        each(low, high, unit)

    def g_rows(k, i, rel):
        return r.gbuf.at[pl.ds(part_row[k] + (position(i) * 2 + rel) * PARTS[k], PARTS[k])]

    def g_direct(k, i):
        slot = seen_from(i)
        return remote(g_rows(k, 0, 0), g_rows(k, slot, 0), r.gd_send.at[k, i], r.gd_recv.at[k, slot], column(i))

    def g_arrival(k, i):
        ref = g_rows(k, i, 0)
        return remote(ref, ref, r.gd_send.at[k, i], r.gd_recv.at[k, i], sib_dev)

    def g_over(k, i, rel=0):
        return remote(g_rows(k, i, rel), g_rows(k, i, 1), r.gs_send.at[k, i], r.gs_recv.at[k, i], sib_dev)

    def make_rows(k):
        n, g = PARTS[k], group[k]
        UNIT = n * g
        matched = msend[k][0].astype(F32)
        for i in range(1, PL):
            swap_m[k].copy(i).wait_recv()
            matched = matched + mrecv[k][i].astype(F32)
        weighted = psend[k][0].astype(F32)
        lanes = lax.broadcasted_iota(jnp.int32, (1, UNIT), 1)
        side = [jnp.logical_and(lanes >= b * n, lanes < (b + 1) * n) for b in range(g)]
        totals = jnp.where(side[0], tsend[k][0], 0.0)
        for i in range(1, PL):
            swap_p[k].copy(i).wait_recv()
            swap_t[k].copy(i).wait_recv()
            weighted = weighted + precv[k][i].astype(F32)
            totals = totals + jnp.where(side[i % g], trecv[k][i], 0.0)
        column_totals = jnp.broadcast_to(totals, (128, UNIT)).T
        total = column_totals[0:n, :]
        for b in range(1, g):
            total = total + column_totals[b * n : (b + 1) * n, :]
        wide = jnp.concatenate([total] * (E // 128), axis=1)
        grad = (weighted / wide - matched) * (1.0 / TEMP)
        unit_rows = ubuf[k][...]
        along = jnp.sum(unit_rows * grad, axis=1, keepdims=True)
        norm = jnp.concatenate([rnbuf[k][...]] * (E // 128), axis=1)
        g_rows(k, 0, 0)[...] = ((grad - unit_rows * along) / norm).astype(BF16)
        g_over(k, 0).start()
        for i in range(1, Z):
            g_direct(k, i).start()
        hit = qbuf[k][0].astype(F32) * matched
        hit = fold_lanes(jnp.sum(hit.reshape(n // 8, 8, E), axis=0))
        logs = jnp.sum(jnp.log(total).reshape(n // 8, 8, 128), axis=0)
        first = lax.broadcasted_iota(jnp.int32, (8, 128), 1) == 0
        return jnp.where(first, logs, 0.0) - hit * (1.0 / TEMP)

    def back(k, *hops):
        for i in places(hops):
            if i:
                g_arrival(k, i).wait_recv()
                g_over(k, i).start()
        for i in places(hops):
            g_over(k, i, 1).wait_recv()
        start, stop = span(k, hops)
        dp = dot_nt(r.whbuf[...], r.gbuf[start:stop, :]) * r.dgt[:, start:stop]
        r.dpt[:, start:stop] = dp.astype(BF16)

    def lp_copy(i):
        return remote(r.lplane.at[pid], r.lplane.at[pid], r.lp_send.at[i], r.lp_recv.at[i], plane(i))

    def lp_arrival(i):
        p = unit_u(i // 2) * 2 + flip(xhi, i % 2)
        return remote(r.lplane.at[p], r.lplane.at[p], r.lp_send.at[i], r.lp_recv.at[i], sib_dev)

    def lc_copy(i):
        ref = r.lcol.at[z]
        return remote(ref, ref, r.lc_send.at[i], r.lc_recv.at[seen_from(i)], column(i))

    def lc_arrival(i):
        ref = r.lcol.at[unit_z(i)]
        return remote(ref, ref, r.lc_send.at[i], r.lc_recv.at[i], sib_dev)

    def ls_copy(c):
        return remote(r.lsib.at[c], r.lsib.at[c], r.ls_send, r.ls_recv, sib_dev)

    for copy in own_copies:
        copy.wait()
    keys_ring.passing_all(1)
    rings[0].begin_with(1)
    rings[0].over_own().start()
    keys_ring.passing_all(2)
    rings[0].passing(1, 0)
    keys_ring.passing_all(3)
    rings[0].passing(1, 1)
    keys_ring.passing_all(4)
    rings[0].passing(2, 0)
    for j in range(1, U):
        pair_copy(j).wait_recv()
    for hop in range(HOPS + 1):
        keys_ring.other_ready(hop)
    find_pairs(0, 0, 2)
    rings[0].passing(2, 1)
    find_pairs(0, 2, 4)
    rings[0].passing(3, 0)
    find_pairs(1, 0, 2)
    rings[0].passing(3, 1)
    rings[1].begin()
    find_pairs(1, 2, 4)
    for copy in w_copies:
        copy.wait_recv()
    encode(0, 1)
    encode(0, 2)
    rings[0].passing_all(4)
    encode(0, 3)
    head_send(0, 1, 2)
    encode(0, 0, 4)
    head_send(0, 3, 0, 4)
    rings[1].passing_all(1)
    rings[1].passing_all(2)
    encode(1, 1)
    rings[1].passing_all(3)
    encode(1, 2)
    make_queries(0)
    rings[1].passing_all(4)
    encode(1, 3)
    encode(1, 0, 4)
    head_send(1, 1, 2, 3, 0, 4)
    attend(0, 0, 4)
    make_queries(1)
    loss = make_rows(0)
    attend(1, 0, 4)
    back(0, 1, 2)
    back(0, 3, 0, 4)
    ghead = dot_nn(r.hidt[:, 0 : part_row[1]], r.gbuf[0 : part_row[1], :])
    loss = loss + make_rows(1)
    r.lplane[pid] = loss
    for i in range(1, PL):
        lp_copy(i).start()
    back(1, 1, 2)
    back(1, 3, 0, 4)

    ghead = ghead + dot_nn(r.hidt[:, part_row[1] :], r.gbuf[part_row[1] :, :])
    r.ghb[...] = ghead.T.astype(BF16)

    def f_copy(j, c):
        slot = j * 2 + jnp.where(holder, 0, 1)
        return remote(
            r.fsend.at[j, c],
            r.frecv.at[slot],
            r.f_send.at[j, c],
            r.f_recv.at[slot],
            (unit_u(j) * 2 + c, z * 2 + core),
        )

    def f_local(j, c):
        return jnp.logical_and(jnp.logical_and(holder, j == 0), c == core)

    def last(step):
        j = U - 1 - step
        n = unit_u(j)
        cols = pl.ds(pl.multiple_of(n * 2 * DS, 2 * DS), 2 * DS)
        part = dot_nn(r.dpt[...], r.xbuf[:, cols]).astype(BF16)
        for c in (0, 1):
            d = n * 2 + c
            r.fsend[j, c, 0:HS, :] = part[:, c * DS : (c + 1) * DS]
            gh = r.ghb[pl.ds(pl.multiple_of(d * ES, 16), ES), :]
            for w in range(HS // 128):
                r.fsend[j, c, HS + w * ES : HS + (w + 1) * ES, :] = gh[:, w * 128 : (w + 1) * 128]

            @pl.when(jnp.logical_not(f_local(j, c)))
            def _():
                f_copy(j, c).start()

            @pl.when(f_local(j, c))
            def _():
                pltpu.make_async_copy(r.fsend.at[j, c], r.frecv.at[0], r.f_recv.at[0]).start()

    each(0, U, last)

    for i in range(1, PL):
        lp_arrival(i).wait_recv()
    loss = r.lplane[0]
    for p in range(1, PL):
        loss = loss + r.lplane[p]
    r.lcol[z] = loss
    for i in range(1, Z):
        lc_copy(i).start()

    for ring in [keys_ring] + rings:
        ring.drain()

    @pl.when(holder)
    def _():
        for copy in w_copies:
            copy.wait_send()

    for j in range(1, U):
        pair_copy(j).wait_send()
    for k in range(K):
        for i in range(Z):
            hs_copy(k, i).wait_send()
            g_over(k, i).wait_send()
            if i:
                hd_copy(k, i).wait_send()
                g_direct(k, i).wait_send()
        for i in range(1, PL):
            swap_q[k].own_copy(i).wait_send()
            swap_m[k].copy(i).wait_send()
            swap_p[k].copy(i).wait_send()
            swap_t[k].copy(i).wait_send()
    for i in range(1, Z):
        lc_arrival(i).wait_recv()
    loss = r.lcol[0]
    for p in range(1, Z):
        loss = loss + r.lcol[p]
    r.lsib[core] = loss
    ls_copy(core).start()
    for i in range(1, PL):
        lp_copy(i).wait_send()
    for i in range(1, Z):
        lc_copy(i).wait_send()

    ls_copy(1 - core).wait_recv()
    ls_copy(core).wait_send()
    loss = r.lsib[0] + r.lsib[1]
    loss = jnp.sum(loss, axis=1, keepdims=True)
    loss = jnp.sum(loss, axis=0, keepdims=True) * (1.0 / TOKENS)
    sums = HS + ES * (HS // 128)
    sums_out[sums : sums + 8, :] = jnp.broadcast_to(loss, (8, DS))

    def f_arrival(s):
        return remote(r.frecv.at[s], r.frecv.at[s], r.f_send.at[0, 0], r.f_recv.at[s], sib_dev)

    each(0, PL, lambda s: f_arrival(s).wait_recv())
    total = r.frecv[0].astype(F32)
    for s in range(1, PL):
        total = total + r.frecv[s].astype(F32)
    sums_out[0:sums, :] = total

    def f_sent(j):
        for c in (0, 1):

            @pl.when(jnp.logical_not(f_local(j, c)))
            def _():
                f_copy(j, c).wait_send()

    each(0, U, f_sent)


def finish(sums, loss_out, gl_out, gh_out):
    HS, (ES, _) = gl_out.shape[1], gh_out.shape
    gl_out[...] = sums[0:HS, :].T
    for w in range(HS // 128):
        gh_out[:, w * 128 : (w + 1) * 128] = sums[HS + w * ES : HS + (w + 1) * ES, :]
    end = HS + ES * (HS // 128)
    loss_out[...] = sums[end : end + 1, 0:1]


def solution(mesh):
    PL = mesh.shape["blk"]
    Z = mesh.shape["grp"] // 2
    M = 2 * Z
    K = len(PARTS)

    def on_device(series, positives, w_last, w_head, pair_index):
        TB, D = series.shape
        HS = w_last.shape[1]
        E = w_head.shape[1]
        DS, ES = D // PL, E // PL
        dims = (Z, PL, TB, D, HS, E, TB * PL * M)
        pair = pair_index.reshape(M, TB)
        vm, sem = pltpu.VMEM, pltpu.SemaphoreType.DMA
        rows = M * TB
        fr = HS + ES * (HS // 128)
        scratch = dict(
            xbuf=vm((rows, D), BF16),
            wbuf=vm((D, HS), BF16),
            whbuf=vm((HS, E), BF16),
            kbuf=vm((rows, E), BF16),
            prbuf=vm((PL // 2, M, TB), jnp.int32),
            hidt=vm((HS, rows), BF16),
            dgt=vm((HS, rows), F32),
            gbuf=vm((rows, E), BF16),
            dpt=vm((HS, rows), BF16),
            ghb=vm((E, HS), BF16),
            fsend=vm((PL // 2, 2, fr, DS), BF16),
            frecv=vm((PL, fr, DS), BF16),
            lplane=vm((PL, 8, 128), F32),
            lcol=vm((Z, 8, 128), F32),
            lsib=vm((2, 8, 128), F32),
            x_sem=sem((K,)),
            ls_send=sem,
            ls_recv=sem,
        )
        for k, n in enumerate(PARTS):
            for name in ("msend", "mrecv", "qbuf", "psend", "precv"):
                scratch[name + str(k)] = vm((PL, n, E), BF16)
            for name in ("tsend", "trecv"):
                scratch[name + str(k)] = vm((PL, 1, n * GROUPS[k]), F32)
            for name in ("hown", "hsend", "hsib"):
                scratch[name + str(k)] = vm((Z, n, E), F32)
            for name in ("hdir", "hrecv"):
                scratch[name + str(k)] = vm((Z, n, E), BF16)
            scratch["ubuf" + str(k)] = vm((n, E), F32)
            scratch["rnbuf" + str(k)] = vm((n, 128), F32)
        hops = Z // 2
        sems = dict(
            w=(2,), pr=(PL // 2,), m=(K, PL), hs=(K, Z), hd=(K, Z), q=(K, PL), p=(K, PL), t=(K, PL),
            gd=(K, Z), gs=(K, Z), lp=(PL,), lc=(Z,), f=(PL // 2, 2),
        )
        for name, chunks in [("k", KEY_CHUNKS)] + [("x%d" % k, c) for k, c in enumerate(CHUNKS)]:
            sems[name] = (2, hops * chunks)
            sems[name + "s"] = (2, hops * chunks + chunks // 2)
        for name, shape in sems.items():
            scratch[name + "_send"] = sem(shape)
            scratch[name + "_recv"] = sem((PL,) if name == "f" else shape)
        names = list(scratch)

        def body(*refs):
            kernel(dims, refs[:5], refs[5:6], types.SimpleNamespace(**dict(zip(names, refs[6:]))))

        any_spec = pl.BlockSpec(memory_space=pl.ANY)
        vm_spec = pl.BlockSpec(memory_space=pltpu.VMEM)
        (sums,) = pl.pallas_call(
            body,
            out_shape=(pltpu.VMEM((fr + 8, DS), F32),),
            in_specs=[any_spec, vm_spec, any_spec, any_spec, vm_spec],
            out_specs=(vm_spec,),
            scratch_shapes=list(scratch.values()),
            compiler_params=pltpu.CompilerParams(
                collective_id=0, has_side_effects=True, vmem_limit_bytes=VMEM_BYTES
            ),
        )(series, positives, w_last, w_head, pair)
        loss, grad_last, grad_head = pl.pallas_call(
            finish,
            out_shape=(
                jax.ShapeDtypeStruct((1, 1), F32),
                jax.ShapeDtypeStruct((DS, HS), F32),
                jax.ShapeDtypeStruct((ES, HS), F32),
            ),
            in_specs=[vm_spec],
            out_specs=(vm_spec, vm_spec, vm_spec),
        )(sums)
        return (loss[0, 0], grad_last, grad_head.T)

    return jax.shard_map(
        on_device,
        mesh=mesh,
        in_specs=(
            P(("blk", "grp"), None),
            P(("blk", "grp"), None),
            P(None, "grp"),
            P("grp", None),
            P("blk"),
        ),
        out_specs=(P(), P("blk", "grp"), P("grp", "blk")),
        check_vma=False,
    )
```
